128 devices in a mesh: wide: 16 (over z, x), narrow: 8 (over y, core).
Axes of the slice: x: 4, y: 4, z: 4, core: 2. Of those that a mesh axis runs over, the one named last changes fastest.
Arguments:
- tokens: bfloat16 [1024, 16384], P(None, ('narrow', 'wide')), may hold values from -6 to 6
- gate_weight: bfloat16 [16384, 26624], P('narrow', 'wide'), may hold values from -0.0625 to 0.0625
- up_weight: bfloat16 [16384, 26624], P('narrow', 'wide'), may hold values from -0.0625 to 0.0625
- down_weight: bfloat16 [26624, 16384], P('wide', 'narrow'), may hold values from -0.0546875 to 0.0546875
Outputs:
- mixed: bfloat16 [1024, 16384], P(None, ('narrow', 'wide'))
The draws below stay inside these ranges and needn't reach their ends.
All inputs are finite; a program needn't handle non-finite values.
Results may differ from the reference program's by a relative error of at most 0.005.
Values may be sent and summed in bfloat16 or wider, within the bound.
No kernel may reach another device: no remote copies, remote signals or barrier semaphores. Data moves between devices by JAX's collectives and lax.ppermute only.
A program may use at most 128 MiB of HBM per device.

```python
import jax
import jax.numpy as jnp

D = 16384
FF = 26624
TOKENS = 1024


def with_spikes(drawn, stream_key, source, target, parts, factor):
    def block_of(dim):
        return (jnp.arange(drawn.shape[dim]) // (drawn.shape[dim] // parts)).reshape((-1,) + (1,) * (drawn.ndim - 1 - dim))

    near = jax.random.permutation(stream_key, parts)[block_of(target)]
    second = (block_of(target) + parts // 2) % parts
    return jnp.where((block_of(source) == near) | (block_of(source) == second), factor * drawn, drawn)


def block_levels(key, extent, pieces, low, largest):
    loudness = 1.0
    for axis_at, blocks in pieces:
        heights = jax.random.uniform(jax.random.fold_in(jax.random.fold_in(key, 6), axis_at), (blocks,), jnp.float32, low / len(pieces), largest / len(pieces))
        loudness = loudness * jnp.repeat(jnp.exp(heights), extent[axis_at] // blocks).reshape((-1,) + (1,) * (len(extent) - 1 - axis_at))
    return loudness


def scatter_about(rng, shape, spread, reach, pieces=(), dtype=jnp.bfloat16):
    array = jax.random.normal(rng, shape, jnp.float32) * spread
    if len(pieces) > 0:
        array = block_levels(rng, shape, pieces, -0.22, 0.18) * array
    return jnp.clip(array, min=-reach, max=reach).astype(dtype)


def noise_with(rng, extent, scale, reach, shards, heavy, held_as=jnp.bfloat16):
    entries = scale * jax.random.normal(rng, extent, jnp.float32)
    if shards:
        entries = entries * block_levels(rng, extent, shards, -0.22, 0.18)
    return jnp.clip(with_spikes(entries, jax.random.fold_in(rng, 3), *heavy), -reach, reach).astype(held_as)


def setup_inputs(seed: int = 0) -> dict:
    key_of = jax.random.split(jax.random.key(seed), 5)
    tokens = scatter_about(key_of[0], (TOKENS, D), 1.0, 6.0, ((1, 128),))
    gate_weight = noise_with(key_of[1], (D, FF), D ** -0.5, 0.0625, ((0, 8), (1, 16)), (0, 1, 16, 2.0))
    up_weight = noise_with(key_of[2], (D, FF), D ** -0.5, 0.0625, ((0, 8), (1, 16)), (0, 1, 16, 2.0))
    down_weight = noise_with(key_of[3], (FF, D), FF ** -0.5, 0.0546875, ((0, 16), (1, 8)), (0, 1, 16, 2.0))
    return {"tokens": tokens, "gate_weight": gate_weight, "up_weight": up_weight, "down_weight": down_weight}


def reference(tokens, gate_weight, up_weight, down_weight):
    gate = jnp.dot(tokens, gate_weight, preferred_element_type=jnp.float32)
    up = jnp.dot(tokens, up_weight, preferred_element_type=jnp.float32)
    hidden = (jax.nn.silu(gate) * up).astype(jnp.bfloat16)
    return jnp.dot(hidden, down_weight, preferred_element_type=jnp.float32).astype(jnp.bfloat16)
```

```python
import functools

import jax
import jax.numpy as jnp
from jax import lax
from jax.experimental import pallas as pl
from jax.experimental.pallas import tpu as pltpu
from jax.sharding import PartitionSpec as P

CHUNKS = 2
LANES = 128
F32, BF16 = jnp.float32, jnp.bfloat16
ANY = pl.BlockSpec(memory_space=pl.ANY)
VMEM = pl.BlockSpec(memory_space=pltpu.VMEM)
SMEM = pl.BlockSpec(memory_space=pltpu.SMEM)


def wide_from(dz, dx):
    return [(((z + dz) % 4) * 4 + (x + dx) % 4, z * 4 + x) for z in range(4) for x in range(4)]


def narrow_from(dy, dc):
    return [(((y + dy) % 4) * 2 + (c + dc) % 2, y * 2 + c) for y in range(4) for c in range(2)]


def on_axis(axis, step):
    return wide_from(step, 0) if axis == "z" else wide_from(0, step)


def gather_wide(rows, first):
    second = "x" if first == "z" else "z"
    line = jnp.stack([rows] + [lax.ppermute(rows, "wide", on_axis(first, s)) for s in (1, 2, 3)])
    return [line] + [lax.ppermute(line, "wide", on_axis(second, s)) for s in (1, 2, 3)]


def block_at(first, z, x, outer, inner):
    if first == "z":
        return lax.rem(z + inner, 4) * 4 + lax.rem(x + outer, 4)
    return lax.rem(z + outer, 4) * 4 + lax.rem(x + inner, 4)


def project_kernel(other, place, *refs):
    halves, (gate_hbm, up_hbm), refs = refs[:8], refs[8:10], refs[10:]
    if other:
        (out,), refs = refs[:1], refs[1:]
    else:
        received, outs, refs = refs[0], refs[1:5], refs[5:]
    staged, lhs, weights, token_sem, weight_sem = refs
    z, x, y, c = place[0], place[1], place[2], place[3]
    half = 1 - c if other else c
    tiles = weights.shape[0]
    units = gate_hbm.shape[1]

    def token_copies(which):
        first = "zx"[which]
        for outer in range(4):
            for inner in range(4):
                columns = pl.ds(pl.multiple_of(block_at(first, z, x, outer, inner) * LANES, LANES), LANES)
                yield pltpu.make_async_copy(
                    halves[which * 4 + outer].at[inner], staged.at[:, columns], token_sem.at[outer * 4 + inner]
                )

    def weight_copies(t):
        columns = pl.ds(pl.multiple_of(t * LANES, LANES), LANES)
        return (
            pltpu.make_async_copy(gate_hbm.at[:, columns], weights.at[t, :, :LANES], weight_sem.at[t, 0]),
            pltpu.make_async_copy(up_hbm.at[:, columns], weights.at[t, :, LANES:], weight_sem.at[t, 1]),
        )

    for which in range(2):
        @pl.when(half == which)
        def _():
            for copy in token_copies(which):
                copy.start()

    @pl.loop(0, tiles)
    def _(t):
        for copy in weight_copies(t):
            copy.start()

    for which in range(2):
        @pl.when(half == which)
        def _():
            for copy in token_copies(which):
                copy.wait()

    quarter = lhs.shape[0] // 4
    for j in range(4):
        rows = pl.ds(pl.multiple_of(lax.rem(y + j, 4) * quarter, quarter), quarter)
        lhs[j * quarter : (j + 1) * quarter, :] = staged[rows, :]

    @pl.loop(0, tiles)
    def _(t):
        for copy in weight_copies(t):
            copy.wait()
        term = jnp.dot(lhs[...], weights[t], preferred_element_type=F32)
        for part in range(2):
            columns = pl.ds(pl.multiple_of(t * LANES + part * units, LANES), LANES)
            block = term[:, part * LANES : (part + 1) * LANES]
            if other:
                out[:, columns] = block.astype(out.dtype)
            else:
                block = block + received[:, columns].astype(F32)
                for j in range(4):
                    outs[j][:, columns] = block[j * quarter : (j + 1) * quarter].astype(outs[j].dtype)


def project(other, place, halves, gate_weight, up_weight, received=None):
    rows = halves[0].shape[1]
    depth, units = gate_weight.shape
    tiles = units // LANES
    if other:
        shapes = [jax.ShapeDtypeStruct((rows, 2 * units), BF16)]
    else:
        shapes = [jax.ShapeDtypeStruct((rows // 4, 2 * units), F32 if j == 0 else BF16) for j in range(4)]
    return pl.pallas_call(
        functools.partial(project_kernel, other),
        out_shape=shapes,
        in_specs=[SMEM] + [ANY] * 10 + ([] if other else [VMEM]),
        out_specs=[VMEM] * len(shapes),
        scratch_shapes=[
            pltpu.VMEM((rows, depth), BF16),
            pltpu.VMEM((rows, depth), BF16),
            pltpu.VMEM((tiles, depth, 2 * LANES), BF16),
            pltpu.SemaphoreType.DMA((16,)),
            pltpu.SemaphoreType.DMA((tiles, 2)),
        ],
        compiler_params=pltpu.CompilerParams(vmem_limit_bytes=40 << 20),
        cost_estimate=pl.CostEstimate(
            flops=4 * rows * depth * units, bytes_accessed=4 * depth * units + 4 * rows * units, transcendentals=0
        ),
        name="project_other" if other else "project_own",
    )(place, *halves, gate_weight, up_weight, *([] if other else [received]))


def hidden_kernel(own, a, b, c, out):
    units = out.shape[1]
    total = own[...] + a[...].astype(F32) + b[...].astype(F32) + c[...].astype(F32)
    gate, up = total[:, :units], total[:, units:]
    out[...] = (gate / (1.0 + jnp.exp(-gate)) * up).astype(BF16)


def hidden_of(parts):
    rows, columns = parts[0].shape
    return pl.pallas_call(
        hidden_kernel,
        out_shape=jax.ShapeDtypeStruct((rows, columns // 2), BF16),
        in_specs=[VMEM] * 4,
        out_specs=VMEM,
        compiler_params=pltpu.CompilerParams(vmem_limit_bytes=40 << 20),
        cost_estimate=pl.CostEstimate(flops=8 * rows * columns, bytes_accessed=11 * rows * columns, transcendentals=rows * columns),
        name="hidden",
    )(*parts)


def down_kernel(first, place, hidden, down_hbm, *refs):
    outs, (weights, sem) = refs[:4], refs[4:]
    z, x = place[0], place[1]

    def copies(outer):
        for inner in range(4):
            block = block_at("x" if first == "z" else "z", z, x, outer, inner)
            columns = pl.ds(pl.multiple_of(block * LANES, LANES), LANES)
            yield pltpu.make_async_copy(
                down_hbm.at[:, columns], weights.at[outer, :, inner * LANES : (inner + 1) * LANES], sem.at[outer * 4 + inner]
            )

    order = (1, 2, 3, 0)
    for outer in order:
        for copy in copies(outer):
            copy.start()
    for outer in order:
        for copy in copies(outer):
            copy.wait()
        outs[outer][...] = jnp.dot(hidden[...], weights[outer], preferred_element_type=F32).astype(outs[outer].dtype)


def down(first, place, hidden, down_weight):
    rows, units = hidden.shape
    width = down_weight.shape[1] // 4
    return pl.pallas_call(
        functools.partial(down_kernel, first),
        out_shape=[jax.ShapeDtypeStruct((rows, width), F32 if j == 0 else BF16) for j in range(4)],
        in_specs=[SMEM, VMEM, ANY],
        out_specs=[VMEM] * 4,
        scratch_shapes=[pltpu.VMEM((4, units, width), BF16), pltpu.SemaphoreType.DMA((16,))],
        compiler_params=pltpu.CompilerParams(vmem_limit_bytes=40 << 20),
        cost_estimate=pl.CostEstimate(
            flops=8 * rows * units * width, bytes_accessed=8 * units * width + 10 * rows * width, transcendentals=0
        ),
        name="down_" + first,
    )(place, hidden, down_weight)


def add_kernel(own, a, b, c, *outs):
    total = own[...] + a[...].astype(F32) + b[...].astype(F32) + c[...].astype(F32)
    for i, out in enumerate(outs):
        out[...] = total[:, i * LANES : (i + 1) * LANES].astype(out.dtype)


def add_line(parts):
    rows, width = parts[0].shape
    return pl.pallas_call(
        add_kernel,
        out_shape=[jax.ShapeDtypeStruct((rows, LANES), F32 if j == 0 else BF16) for j in range(4)],
        in_specs=[VMEM] * 4,
        out_specs=[VMEM] * 4,
        compiler_params=pltpu.CompilerParams(vmem_limit_bytes=40 << 20),
        cost_estimate=pl.CostEstimate(flops=3 * rows * width, bytes_accessed=12 * rows * width, transcendentals=0),
        name="add_line",
    )(*parts)


def last_kernel(place, *refs):
    parts, out = refs[:-1], refs[-1]
    y, c = place[2], place[3]
    half = parts[0].shape[0]
    quarter = half // 4
    for at in range(len(parts) // 4):
        own, *others = parts[at * 4 : at * 4 + 4]
        total = own[...]
        for other in others:
            total = total + other[...].astype(F32)
        total = total.astype(out.dtype)
        side = c if at % 2 == 0 else 1 - c
        for j in range(4):
            start = (at // 2) * 2 * half + side * half + lax.rem(y + j, 4) * quarter
            out[pl.ds(pl.multiple_of(start, quarter), quarter), :] = total[j * quarter : (j + 1) * quarter]


def last(place, parts):
    half = parts[0].shape[0]
    rows = len(parts) // 4 * half
    return pl.pallas_call(
        last_kernel,
        out_shape=jax.ShapeDtypeStruct((rows, LANES), BF16),
        in_specs=[SMEM] + [VMEM] * len(parts),
        out_specs=VMEM,
        compiler_params=pltpu.CompilerParams(vmem_limit_bytes=40 << 20),
        cost_estimate=pl.CostEstimate(flops=3 * rows * LANES, bytes_accessed=12 * rows * LANES, transcendentals=0),
        name="last",
    )(place, *parts)


def send(parts, axis, pairs):
    return [parts[0]] + [lax.ppermute(parts[s], axis, pairs(-s)) for s in (1, 2, 3)]


def body(tokens, gate_weight, up_weight, down_weight):
    wide, narrow = lax.axis_index("wide"), lax.axis_index("narrow")
    place = jnp.stack([wide // 4, wide % 4, narrow // 2, narrow % 2]).astype(jnp.int32)
    half = tokens.shape[0] // CHUNKS // 2
    pieces = [
        [
            part
            for side in range(2)
            for part in gather_wide(lax.slice_in_dim(tokens, (2 * at + side) * half, (2 * at + side + 1) * half), "zx"[side])
        ]
        for at in range(CHUNKS)
    ]
    swap = lambda array: lax.ppermute(array, "narrow", narrow_from(0, 1))
    along_y = lambda step: narrow_from(step, 0)
    finals = []
    for at in range(CHUNKS):
        (others,) = project(True, place, pieces[at], gate_weight, up_weight)
        sums = project(False, place, pieces[at], gate_weight, up_weight, swap(others))
        hidden = hidden_of(send(sums, "narrow", along_y))
        mine = jnp.concatenate([hidden] + [lax.ppermute(hidden, "narrow", along_y(s)) for s in (1, 2, 3)])
        for first, second, rows in (("z", "x", mine), ("x", "z", swap(mine))):
            partials = down(first, place, rows, down_weight)
            line = add_line(send(partials, "wide", functools.partial(on_axis, first)))
            finals += send(line, "wide", functools.partial(on_axis, second))
    return last(place, finals)


def solution(mesh):
    return jax.shard_map(
        body,
        mesh=mesh,
        in_specs=(
            P(None, ("narrow", "wide")),
            P("narrow", "wide"),
            P("narrow", "wide"),
            P("wide", "narrow"),
        ),
        out_specs=P(None, ("narrow", "wide")),
        check_vma=False,
    )
```

```python
import functools

import jax
import jax.numpy as jnp
from jax import lax
from jax.experimental import pallas as pl
from jax.experimental.pallas import tpu as pltpu
from jax.sharding import PartitionSpec as P

LANES = 128
LIMIT = 16 << 20
F32, BF16 = jnp.float32, jnp.bfloat16
VMEM = pl.BlockSpec(memory_space=pltpu.VMEM)
SMEM = pl.BlockSpec(memory_space=pltpu.SMEM)
HBM = pl.BlockSpec(memory_space=pltpu.HBM)


def from_wide(axis, step, array):
    dz, dx = (step, 0) if axis == "z" else (0, step)
    pairs = [(((z + dz) % 4) * 4 + (x + dx) % 4, z * 4 + x) for z in range(4) for x in range(4)]
    return lax.ppermute(array, "wide", pairs)


def from_narrow(dy, dc, array):
    pairs = [(((y + dy) % 4) * 2 + (c + dc) % 2, y * 2 + c) for y in range(4) for c in range(2)]
    return lax.ppermute(array, "narrow", pairs)


def from_y(step, array):
    return from_narrow(step, 0, array)


def swap(array):
    return from_narrow(0, 1, array)


def after(value, *earlier):
    return lax.optimization_barrier((value, *earlier))[0]


def call(kernel, name, out_shape, in_specs, operands, scratch=(), micros=1, many=True):
    return pl.pallas_call(
        kernel,
        out_shape=out_shape,
        in_specs=in_specs,
        out_specs=[VMEM] * len(out_shape) if many else VMEM,
        scratch_shapes=scratch,
        compiler_params=pltpu.CompilerParams(vmem_limit_bytes=LIMIT),
        cost_estimate=pl.CostEstimate(flops=micros * 10**9, bytes_accessed=0, transcendentals=0),
        name=name,
    )(*operands)


def load_kernel(*refs):
    count = len(refs) // 2
    copies = [pltpu.make_async_copy(refs[i], refs[count + i], refs[-1].at[i]) for i in range(count)]
    for copy in copies:
        copy.start()
    for copy in copies:
        copy.wait()


def load(*arrays):
    out = call(
        load_kernel,
        "load",
        [pltpu.VMEM(a.shape, a.dtype) for a in arrays],
        [HBM] * len(arrays),
        [pltpu.with_memory_space_constraint(a, pltpu.HBM) for a in arrays],
        scratch=[pltpu.SemaphoreType.DMA((len(arrays),))],
        micros=5,
    )
    return [pltpu.with_memory_space_constraint(a, pltpu.VMEM) for a in out]


def line_of(axis, rows):
    near = [from_wide(axis, 1, rows), from_wide(axis, -1, rows), from_wide(axis, 2, rows)]
    return [rows, near[0], near[2], near[1]]


def plane_of(axis, line):
    ahead, behind = from_wide(axis, 1, line), from_wide(axis, -1, line)
    return [line, ahead, from_wide(axis, -1, behind[:2]), from_wide(axis, 1, ahead[2:]), behind]


def assemble_kernel(first, place, own, ahead, opposite_a, opposite_b, behind, out):
    z, x, y, c = place[0], place[1], place[2], place[3]
    block = out.shape[0] // 8
    for outer in range(4):
        for inner in range(4):
            if first == "z":
                column = lax.rem(z + inner, 4) * 4 + lax.rem(x + outer, 4)
            else:
                column = lax.rem(z + outer, 4) * 4 + lax.rem(x + inner, 4)
            columns = pl.ds(pl.multiple_of(column * LANES, LANES), LANES)
            if outer == 2:
                part, index = (opposite_a, inner) if inner < 2 else (opposite_b, inner - 2)
            else:
                part, index = (own, ahead, None, behind)[outer], inner
            for side in range(2):
                core = 1 - c if side == 0 else c
                for j in range(4):
                    rows = pl.ds(pl.multiple_of((lax.rem(y + j, 4) * 2 + core) * block, block), block)
                    at = (side * 4 + j) * block
                    out[at : at + block, columns] = part[index, rows, :]


def assemble(first, place, parts, rows, depth):
    return call(
        functools.partial(assemble_kernel, first),
        "assemble_" + first,
        jax.ShapeDtypeStruct((rows, depth), BF16),
        [SMEM] + [VMEM] * len(parts),
        [place, *parts],
        many=False,
    )


def project_other_kernel(rows, gate_weight, up_weight, out):
    units = gate_weight.shape[1]
    half = rows.shape[0] // 2
    for t in range(0, units, LANES):
        weights = jnp.concatenate([gate_weight[:, t : t + LANES], up_weight[:, t : t + LANES]], axis=1)
        term = jnp.dot(rows[:half, :], weights, preferred_element_type=F32)
        out[:, t : t + LANES] = term[:, :LANES]
        out[:, units + t : units + t + LANES] = term[:, LANES:]


def project_other(rows, gate_weight, up_weight):
    half = rows.shape[0] // 2
    units = gate_weight.shape[1]
    shape = jax.ShapeDtypeStruct((half, 2 * units), F32)
    return call(
        project_other_kernel, "project_other", shape, [VMEM] * 3, [rows, gate_weight, up_weight], micros=4, many=False
    )


def project_own_kernel(rows, gate_weight, up_weight, received, own, to_ahead, to_behind, keep_ahead, keep_behind):
    units = gate_weight.shape[1]
    half = rows.shape[0] // 2
    quarter = half // 4
    eighth = quarter // 2
    for t in range(0, units, LANES):
        weights = jnp.concatenate([gate_weight[:, t : t + LANES], up_weight[:, t : t + LANES]], axis=1)
        term = jnp.dot(rows[half:, :], weights, preferred_element_type=F32)
        for part in range(2):
            columns = slice(t + part * units, t + part * units + LANES)
            block = term[:, part * LANES : (part + 1) * LANES] + received[:, columns]
            at = lambda j, h: block[j * quarter + h * eighth : j * quarter + (h + 1) * eighth]
            own[:, columns] = block[:quarter]
            to_ahead[:eighth, columns] = at(2, 0).astype(BF16)
            to_ahead[eighth:, columns] = at(1, 1).astype(BF16)
            to_behind[:eighth, columns] = at(2, 1).astype(BF16)
            to_behind[eighth:, columns] = at(3, 0).astype(BF16)
            keep_ahead[:, columns] = at(1, 0)
            keep_behind[:, columns] = at(3, 1)


def project_own(rows, gate_weight, up_weight, received):
    half = rows.shape[0] // 2
    units = gate_weight.shape[1]
    shapes = [
        jax.ShapeDtypeStruct((count, 2 * units), dtype)
        for count, dtype in ((half // 4, F32), (half // 4, BF16), (half // 4, BF16), (half // 8, F32), (half // 8, F32))
    ]
    return call(project_own_kernel, "project_own", shapes, [VMEM] * 4, [rows, gate_weight, up_weight, received], micros=4)


def relay_kernel(keep_ahead, keep_behind, from_behind, from_ahead, to_ahead, to_behind):
    eighth = keep_ahead.shape[0]
    to_ahead[...] = (keep_ahead[...] + from_behind[:eighth, :].astype(F32)).astype(BF16)
    to_behind[...] = (keep_behind[...] + from_ahead[:eighth, :].astype(F32)).astype(BF16)


def hidden_kernel(own, from_behind, from_ahead, relay_behind, relay_ahead, out):
    units = out.shape[1]
    eighth = out.shape[0] // 2
    for h in range(2):
        rows = slice(h * eighth, (h + 1) * eighth)
        behind = relay_behind[...] if h == 0 else from_behind[eighth:, :]
        ahead = relay_ahead[...] if h == 1 else from_ahead[eighth:, :]
        total = own[rows, :] + behind.astype(F32) + ahead.astype(F32)
        gate, up = total[:, :units], total[:, units:]
        out[rows, :] = (gate / (1.0 + jnp.exp(-gate)) * up).astype(BF16)


def relay(parts, from_behind, from_ahead):
    keeps = parts[3:]
    shape = jax.ShapeDtypeStruct(keeps[0].shape, BF16)
    return call(relay_kernel, "relay", [shape] * 2, [VMEM] * 4, [*keeps, from_behind, from_ahead])


def hidden_of(parts):
    rows, columns = parts[0].shape
    return call(
        hidden_kernel, "hidden", jax.ShapeDtypeStruct((rows, columns // 2), BF16), [VMEM] * 5, parts, many=False
    )


def down_kernel(first, place, rows, down_weight, own, to_ahead, to_behind, keep_ahead, keep_behind):
    z, x = place[0], place[1]
    half = rows.shape[0] // 2
    for outer in (2, 1, 3, 0):
        for pair in (0, 2):
            weights = []
            for inner in (pair, pair + 1):
                dz, dx = (outer, inner) if first == "z" else (inner, outer)
                column = (lax.rem(z + dz, 4) * 4 + lax.rem(x + dx, 4)) * LANES
                weights.append(down_weight[:, pl.ds(pl.multiple_of(column, LANES), LANES)])
            term = jnp.dot(rows[...], jnp.concatenate(weights, axis=1), preferred_element_type=F32)
            columns = slice(pair * LANES, (pair + 2) * LANES)
            if outer == 0:
                own[:, columns] = term
            elif outer == 1:
                keep_ahead[:, columns] = term[:half]
                to_ahead[half:, columns] = term[half:].astype(BF16)
            elif outer == 2:
                to_ahead[:half, columns] = term[:half].astype(BF16)
                to_behind[:half, columns] = term[half:].astype(BF16)
            else:
                to_behind[half:, columns] = term[:half].astype(BF16)
                keep_behind[:, columns] = term[half:]


def down(first, place, rows, down_weight):
    count = rows.shape[0]
    width = down_weight.shape[1] // 4
    shapes = [
        jax.ShapeDtypeStruct((n, width), dtype)
        for n, dtype in ((count, F32), (count, BF16), (count, BF16), (count // 2, F32), (count // 2, F32))
    ]
    return call(
        functools.partial(down_kernel, first),
        "down_" + first,
        shapes,
        [SMEM, VMEM, VMEM],
        [place, rows, down_weight],
        micros=4,
    )


def add_kernel(own, from_behind, from_ahead, relay_behind, relay_ahead, *outs):
    half = relay_behind.shape[0]
    for h in range(2):
        rows = slice(h * half, (h + 1) * half)
        behind = relay_behind[...] if h == 0 else from_behind[half:, :]
        ahead = relay_ahead[...] if h == 1 else from_ahead[half:, :]
        total = own[rows, :] + behind.astype(F32) + ahead.astype(F32)
        for i, out in enumerate(outs):
            out[rows, :] = total[:, i * LANES : (i + 1) * LANES].astype(out.dtype)


def add_line(parts):
    shapes = [jax.ShapeDtypeStruct((parts[0].shape[0], LANES), F32 if j == 0 else BF16) for j in range(4)]
    return call(add_kernel, "add_line", shapes, [VMEM] * 5, parts)


def send(axis, parts):
    return [parts[0], from_wide(axis, -1, parts[1]), from_wide(axis, -2, parts[2]), from_wide(axis, -3, parts[3])]


def last_kernel(place, *refs):
    parts, out = refs[:-1], refs[-1]
    y, c = place[2], place[3]
    rows = parts[0].shape[0]
    block = rows // 8
    for chunk in range(2):
        total = parts[4 * chunk][...]
        for k in range(1, 4):
            total = total + parts[4 * chunk + k][...].astype(F32)
        total = total.astype(BF16)
        for side in range(2):
            core = c if side == 0 else 1 - c
            for j in range(4):
                at = chunk * rows + (lax.rem(y + j, 4) * 2 + core) * block
                value = total[(side * 4 + j) * block : (side * 4 + j + 1) * block]
                out[pl.ds(pl.multiple_of(at, block), block), :] = value


def last(place, parts):
    shape = jax.ShapeDtypeStruct((2 * parts[0].shape[0], LANES), BF16)
    return call(last_kernel, "last", shape, [SMEM] + [VMEM] * 8, [place, *parts], many=False)


def body(tokens, gate_weight, up_weight, down_weight):
    wide, narrow = lax.axis_index("wide"), lax.axis_index("narrow")
    place = jnp.stack([wide // 4, wide % 4, narrow // 2, narrow % 2]).astype(jnp.int32)
    depth = gate_weight.shape[0]
    rows = tokens.shape[0] // 2
    both = range(2)
    tokens = after(tokens, place)
    lines = [line_of(axis, tokens[at * rows : (at + 1) * rows]) for at, axis in enumerate("zx")]
    lines = lax.optimization_barrier(lines)
    lines = [jnp.stack(line) for line in lines]
    nexts = [(from_wide(axis, 1, line), from_wide(axis, -1, line)) for axis, line in zip("xz", lines)]
    nexts = lax.optimization_barrier(nexts)
    planes = [
        [line, ahead, from_wide(axis, -1, behind[:2]), from_wide(axis, 1, ahead[2:]), behind]
        for axis, line, (ahead, behind) in zip("xz", lines, nexts)
    ]
    *weights, down_weight = load(*after((gate_weight, up_weight, down_weight), nexts))
    chunks = [assemble(axis, place, plane, rows, depth) for axis, plane in zip("zx", planes)]
    others = []
    for at in both:
        others.append(project_other(after(chunks[at], *others), *weights))
    received = [swap(array) for array in others]
    parts = []
    for at in both:
        parts.append(project_own(after(chunks[at], others[1], *[p[0] for p in parts]), *weights, received[at]))
    behind = [from_y(-1, p[1]) for p in parts]
    ahead = [from_y(1, p[2]) for p in parts]
    relays = []
    for at in both:
        relays.append(relay(parts[at], after(behind[at], parts[1][0], *[r[0] for r in relays]), ahead[at]))
    seconds = [(from_y(-1, r[0]), from_y(1, r[1])) for r in relays]
    hidden = []
    for at in both:
        second = after(seconds[at][0], relays[1][0], *hidden)
        hidden.append(hidden_of([parts[at][0], behind[at], ahead[at], second, seconds[at][1]]))
    half = hidden[0].shape[0] // 2
    nexts = lax.optimization_barrier([(from_y(1, h), from_y(-1, h)) for h in hidden])
    opposites = [(from_y(-1, behind[:half]), from_y(1, ahead[half:])) for ahead, behind in nexts]
    mine = [jnp.concatenate([h, n[0], *o, n[1]]) for h, n, o in zip(hidden, nexts, opposites)]
    mine[1] = after(mine[1], mine[0])
    all_rows = [jnp.concatenate([m, swap(m)]) for m in mine]
    parts = []
    for at, axis in enumerate("zx"):
        parts.append(down(axis, place, after(all_rows[at], *[p[0] for p in parts]), down_weight))
    behind = [from_wide(axis, -1, p[1]) for axis, p in zip("zx", parts)]
    ahead = [from_wide(axis, 1, p[2]) for axis, p in zip("zx", parts)]
    relays = []
    for at in both:
        relays.append(relay(parts[at], after(behind[at], parts[1][0], *[r[0] for r in relays]), ahead[at]))
    finals = []
    for at, (axis, other) in enumerate(("zx", "xz")):
        second = from_wide(axis, -1, relays[at][0]), from_wide(axis, 1, relays[at][1])
        line = add_line([parts[at][0], behind[at], ahead[at], after(second[0], relays[1][0], *finals[:1]), second[1]])
        finals += send(other, line)
    return last(place, finals)


def solution(mesh):
    return jax.shard_map(
        body,
        mesh=mesh,
        in_specs=(
            P(None, ("narrow", "wide")),
            P("narrow", "wide"),
            P("narrow", "wide"),
            P("wide", "narrow"),
        ),
        out_specs=P(None, ("narrow", "wide")),
        check_vma=False,
    )
```

```python
import functools

import jax
import jax.numpy as jnp
from jax import lax
from jax.experimental import pallas as pl
from jax.experimental.pallas import tpu as pltpu
from jax.sharding import PartitionSpec as P

LANES = 128
LIMIT = 16 << 20
F32, BF16 = jnp.float32, jnp.bfloat16
VMEM = pl.BlockSpec(memory_space=pltpu.VMEM)
SMEM = pl.BlockSpec(memory_space=pltpu.SMEM)
HBM = pl.BlockSpec(memory_space=pltpu.HBM)


def from_wide(axis, bits, array):
    step = bits * 4 if axis == "z" else bits
    return lax.ppermute(array, "wide", [(i ^ step, i) for i in range(16)])


def from_y(bits, array):
    return lax.ppermute(array, "narrow", [(i ^ (bits * 2), i) for i in range(8)])


def swap(array):
    return lax.ppermute(array, "narrow", [(i ^ 1, i) for i in range(8)])


def after(value, *earlier):
    return lax.optimization_barrier((value, *earlier))[0]


def call(kernel, name, out_shape, in_specs, operands, scratch=(), micros=0, many=True):
    return pl.pallas_call(
        kernel,
        out_shape=out_shape,
        in_specs=in_specs,
        out_specs=[VMEM] * len(out_shape) if many else VMEM,
        scratch_shapes=scratch,
        compiler_params=pltpu.CompilerParams(vmem_limit_bytes=LIMIT),
        cost_estimate=pl.CostEstimate(flops=micros * 10**9, bytes_accessed=0, transcendentals=0),
        name=name,
    )(*operands)


def load_kernel(*refs):
    count = len(refs) // 2
    copies = [pltpu.make_async_copy(refs[i], refs[count + i], refs[-1].at[i]) for i in range(count)]
    for copy in copies:
        copy.start()
    for copy in copies:
        copy.wait()


def load(*arrays):
    out = call(
        load_kernel,
        "load",
        [pltpu.VMEM(a.shape, a.dtype) for a in arrays],
        [HBM] * len(arrays),
        [pltpu.with_memory_space_constraint(a, pltpu.HBM) for a in arrays],
        scratch=[pltpu.SemaphoreType.DMA((len(arrays),))],
        micros=5,
    )
    return [pltpu.with_memory_space_constraint(a, pltpu.VMEM) for a in out]


def line_of(axis, rows):
    one, three, two = (from_wide(axis, bits, rows) for bits in (1, 3, 2))
    return [rows, one, two, three]


def assemble_kernel(first, place, own, one, two_a, two_b, three, out):
    z, x, y, c = place[0], place[1], place[2], place[3]
    block = out.shape[0] // 8
    for outer in range(4):
        for inner in range(4):
            if first == "z":
                column = (z ^ inner) * 4 + (x ^ outer)
            else:
                column = (z ^ outer) * 4 + (x ^ inner)
            columns = pl.ds(pl.multiple_of(column * LANES, LANES), LANES)
            if outer == 2:
                part, index = (two_a, inner) if inner < 2 else (two_b, inner - 2)
            else:
                part, index = (own, one, None, three)[outer], inner
            for side in range(2):
                core = 1 - c if side == 0 else c
                for j in range(4):
                    rows = pl.ds(pl.multiple_of(((y ^ j) * 2 + core) * block, block), block)
                    at = (side * 4 + j) * block
                    out[at : at + block, columns] = part[index, rows, :]


def assemble(first, place, parts, rows, depth):
    return call(
        functools.partial(assemble_kernel, first),
        "assemble_" + first,
        jax.ShapeDtypeStruct((rows, depth), BF16),
        [SMEM] + [VMEM] * len(parts),
        [place, *parts],
        many=False,
    )


def project_other_kernel(rows, gate_weight, up_weight, out):
    units = gate_weight.shape[1]
    half = rows.shape[0] // 2
    for t in range(0, units, LANES):
        weights = jnp.concatenate([gate_weight[:, t : t + LANES], up_weight[:, t : t + LANES]], axis=1)
        term = jnp.dot(rows[:half, :], weights, preferred_element_type=F32)
        out[:, t : t + LANES] = term[:, :LANES]
        out[:, units + t : units + t + LANES] = term[:, LANES:]


def project_other(rows, gate_weight, up_weight):
    half = rows.shape[0] // 2
    units = gate_weight.shape[1]
    shape = jax.ShapeDtypeStruct((half, 2 * units), F32)
    return call(
        project_other_kernel, "project_other", shape, [VMEM] * 3, [rows, gate_weight, up_weight], micros=4, many=False
    )


def project_own_kernel(rows, gate_weight, up_weight, received, own, to_one, to_three, keep_one, keep_three):
    units = gate_weight.shape[1]
    half = rows.shape[0] // 2
    quarter = half // 4
    eighth = quarter // 2
    for t in range(0, units, LANES):
        weights = jnp.concatenate([gate_weight[:, t : t + LANES], up_weight[:, t : t + LANES]], axis=1)
        term = jnp.dot(rows[half:, :], weights, preferred_element_type=F32)
        for part in range(2):
            columns = slice(t + part * units, t + part * units + LANES)
            block = term[:, part * LANES : (part + 1) * LANES] + received[:, columns]
            at = lambda j, h: block[j * quarter + h * eighth : j * quarter + (h + 1) * eighth]
            own[:, columns] = block[:quarter]
            to_one[:eighth, columns] = at(2, 0).astype(BF16)
            to_one[eighth:, columns] = at(1, 0).astype(BF16)
            to_three[:eighth, columns] = at(2, 1).astype(BF16)
            to_three[eighth:, columns] = at(3, 1).astype(BF16)
            keep_one[:, columns] = at(1, 1)
            keep_three[:, columns] = at(3, 0)


def project_own(rows, gate_weight, up_weight, received):
    half = rows.shape[0] // 2
    units = gate_weight.shape[1]
    shapes = [
        jax.ShapeDtypeStruct((count, 2 * units), dtype)
        for count, dtype in ((half // 4, F32), (half // 4, BF16), (half // 4, BF16), (half // 8, F32), (half // 8, F32))
    ]
    return call(project_own_kernel, "project_own", shapes, [VMEM] * 4, [rows, gate_weight, up_weight, received], micros=4)


def relay_kernel(keep_one, keep_three, from_one, from_three, to_one, to_three):
    half = keep_one.shape[0]
    to_one[...] = (keep_one[...] + from_three[:half, :].astype(F32)).astype(BF16)
    to_three[...] = (keep_three[...] + from_one[:half, :].astype(F32)).astype(BF16)


def relay(parts, from_one, from_three):
    keeps = parts[3:]
    shape = jax.ShapeDtypeStruct(keeps[0].shape, BF16)
    return call(relay_kernel, "relay", [shape] * 2, [VMEM] * 4, [*keeps, from_one, from_three])


def sum_of(h, own, from_one, from_three, relay_one, relay_three):
    half = relay_one.shape[0]
    direct, relayed = (from_one, relay_three) if h == 0 else (from_three, relay_one)
    return own[h * half : (h + 1) * half, :] + direct[half:, :].astype(F32) + relayed[...].astype(F32)


def hidden_kernel(*refs):
    parts, out = refs[:-1], refs[-1]
    units = out.shape[1]
    half = out.shape[0] // 2
    for h in range(2):
        total = sum_of(h, *parts)
        gate, up = total[:, :units], total[:, units:]
        out[h * half : (h + 1) * half, :] = (gate / (1.0 + jnp.exp(-gate)) * up).astype(BF16)


def hidden_of(parts):
    rows, columns = parts[0].shape
    return call(
        hidden_kernel, "hidden", jax.ShapeDtypeStruct((rows, columns // 2), BF16), [VMEM] * 5, parts, many=False
    )


def down_kernel(first, place, rows, down_weight, own, to_one, to_three, keep_one, keep_three):
    z, x = place[0], place[1]
    half = rows.shape[0] // 2
    for outer in (2, 1, 3, 0):
        for pair in (0, 2):
            weights = []
            for inner in (pair, pair + 1):
                dz, dx = (outer, inner) if first == "z" else (inner, outer)
                column = ((z ^ dz) * 4 + (x ^ dx)) * LANES
                weights.append(down_weight[:, pl.ds(pl.multiple_of(column, LANES), LANES)])
            term = jnp.dot(rows[...], jnp.concatenate(weights, axis=1), preferred_element_type=F32)
            columns = slice(pair * LANES, (pair + 2) * LANES)
            if outer == 0:
                own[:, columns] = term
            elif outer == 1:
                to_one[half:, columns] = term[:half].astype(BF16)
                keep_one[:, columns] = term[half:]
            elif outer == 2:
                to_one[:half, columns] = term[:half].astype(BF16)
                to_three[:half, columns] = term[half:].astype(BF16)
            else:
                keep_three[:, columns] = term[:half]
                to_three[half:, columns] = term[half:].astype(BF16)


def down(first, place, rows, down_weight):
    count = rows.shape[0]
    width = down_weight.shape[1] // 4
    shapes = [
        jax.ShapeDtypeStruct((n, width), dtype)
        for n, dtype in ((count, F32), (count, BF16), (count, BF16), (count // 2, F32), (count // 2, F32))
    ]
    return call(
        functools.partial(down_kernel, first),
        "down_" + first,
        shapes,
        [SMEM, VMEM, VMEM],
        [place, rows, down_weight],
        micros=4,
    )


def add_kernel(own, from_one, from_three, relay_one, relay_three, *outs):
    half = relay_one.shape[0]
    for h in range(2):
        total = sum_of(h, own, from_one, from_three, relay_one, relay_three)
        for i, out in enumerate(outs):
            out[h * half : (h + 1) * half, :] = total[:, i * LANES : (i + 1) * LANES].astype(out.dtype)


def add_line(parts):
    shapes = [jax.ShapeDtypeStruct((parts[0].shape[0], LANES), F32 if j == 0 else BF16) for j in range(4)]
    return call(add_kernel, "add_line", shapes, [VMEM] * 5, parts)


def send(axis, parts):
    return [parts[0]] + [from_wide(axis, bits, parts[bits]) for bits in (1, 2, 3)]


def last_kernel(place, *refs):
    parts, out = refs[:-1], refs[-1]
    y, c = place[2], place[3]
    rows = parts[0].shape[0]
    block = rows // 8
    for chunk in range(2):
        total = parts[4 * chunk][...]
        for k in range(1, 4):
            total = total + parts[4 * chunk + k][...].astype(F32)
        total = total.astype(BF16)
        for side in range(2):
            core = c if side == 0 else 1 - c
            for j in range(4):
                at = chunk * rows + ((y ^ j) * 2 + core) * block
                value = total[(side * 4 + j) * block : (side * 4 + j + 1) * block]
                out[pl.ds(pl.multiple_of(at, block), block), :] = value


def last(place, parts):
    shape = jax.ShapeDtypeStruct((2 * parts[0].shape[0], LANES), BF16)
    return call(last_kernel, "last", shape, [SMEM] + [VMEM] * 8, [place, *parts], many=False)


def body(tokens, gate_weight, up_weight, down_weight):
    wide, narrow = lax.axis_index("wide"), lax.axis_index("narrow")
    place = jnp.stack([wide // 4, wide % 4, narrow // 2, narrow % 2]).astype(jnp.int32)
    depth = gate_weight.shape[0]
    rows = tokens.shape[0] // 2
    both = range(2)
    tokens = after(tokens, place)
    lines = [line_of(axis, tokens[at * rows : (at + 1) * rows]) for at, axis in enumerate("zx")]
    lines[0] = after(lines[0], lines[1][1])
    stacks = [jnp.stack(line) for line in lines]
    nexts = [[from_wide(axis, bits, stack) for bits in (1, 3)] for axis, stack in zip("xz", stacks)]
    *weights, down_weight = load(*after((gate_weight, up_weight, down_weight), stacks))
    nexts[0] = after(nexts[0], down_weight)
    planes = [
        [stack, one, from_wide(axis, 1, three[:2]), from_wide(axis, 3, one[2:]), three]
        for axis, stack, (one, three) in zip("xz", stacks, nexts)
    ]
    chunks = [assemble(axis, place, plane, rows, depth) for axis, plane in zip("zx", planes)]
    others = []
    for at in both:
        others.append(project_other(after(chunks[at], *others), *weights))
    received = [swap(array) for array in others]
    parts = []
    for at in both:
        parts.append(project_own(after(chunks[at], others[1], *[p[0] for p in parts]), *weights, received[at]))
    def first_round(exchange, parts):
        return exchange(1, parts[1]), exchange(3, parts[2])

    def second_round(exchange, pair):
        return exchange(1, pair[0]), exchange(3, pair[1])

    together = lax.optimization_barrier
    half = parts[0][0].shape[0] // 2
    first = [first_round(from_y, p) for p in parts]
    second = [second_round(from_y, relay(parts[0], *after(first[0], parts[1][0]))), None]
    first[1], second[0] = together((first[1], second[0]))
    hidden = [hidden_of([parts[0][0], *first[0], *second[0]]), None]
    near = [[from_y(bits, hidden[0]) for bits in (1, 3)], None]
    second[1] = second_round(from_y, relay(parts[1], *first[1]))
    near[0], second[1] = together((near[0], second[1]))
    hidden[1] = hidden_of([parts[1][0], *first[1], *second[1]])
    near[1] = [from_y(bits, hidden[1]) for bits in (1, 3)]
    far = [second_round(from_y, (near[0][1][:half], near[0][0][half:])), None]
    near[1], far[0] = together((near[1], far[0]))
    parts = []
    for at, axis in enumerate("zx"):
        if at == 1:
            far[1] = after(second_round(from_y, (near[1][1][:half], near[1][0][half:])), parts[0][0])
        rows_here = jnp.concatenate([hidden[at], near[at][0], *far[at], near[at][1]])
        parts.append(down(axis, place, jnp.concatenate([rows_here, swap(rows_here)]), down_weight))
    along = [functools.partial(from_wide, axis) for axis in "zx"]
    first = [first_round(exchange, p) for exchange, p in zip(along, parts)]
    second[0] = second_round(along[0], relay(parts[0], *after(first[0], parts[1][0])))
    first[1], second[0] = together((first[1], second[0]))
    second[1] = second_round(along[1], relay(parts[1], *first[1]))
    final = send("x", add_line([parts[0][0], *first[0], *second[0]]))
    second[1], final = together((second[1], final))
    return last(place, final + send("z", add_line([parts[1][0], *first[1], *second[1]])))


def solution(mesh):
    return jax.shard_map(
        body,
        mesh=mesh,
        in_specs=(
            P(None, ("narrow", "wide")),
            P("narrow", "wide"),
            P("narrow", "wide"),
            P("wide", "narrow"),
        ),
        out_specs=P(None, ("narrow", "wide")),
        check_vma=False,
    )
```

```python
import functools

import jax
import jax.numpy as jnp
from jax import lax
from jax.experimental import pallas as pl
from jax.experimental.pallas import tpu as pltpu
from jax.sharding import PartitionSpec as P

LANES = 128
LIMIT = 16 << 20
F32, BF16 = jnp.float32, jnp.bfloat16
VMEM = pl.BlockSpec(memory_space=pltpu.VMEM)
SMEM = pl.BlockSpec(memory_space=pltpu.SMEM)
HBM = pl.BlockSpec(memory_space=pltpu.HBM)


def from_wide(axis, bits, array):
    step = bits * 4 if axis == "z" else bits
    return lax.ppermute(array, "wide", [(i ^ step, i) for i in range(16)])


def from_y(bits, array):
    return lax.ppermute(array, "narrow", [(i ^ (bits * 2), i) for i in range(8)])


def swap(array):
    return lax.ppermute(array, "narrow", [(i ^ 1, i) for i in range(8)])


def after(value, *earlier):
    return lax.optimization_barrier((value, *earlier))[0]


def call(kernel, name, out_shape, in_specs, operands, scratch=(), micros=0, many=True, aliases={}):
    return pl.pallas_call(
        kernel,
        out_shape=out_shape,
        in_specs=in_specs,
        out_specs=[VMEM] * len(out_shape) if many else VMEM,
        scratch_shapes=scratch,
        input_output_aliases=aliases,
        compiler_params=pltpu.CompilerParams(vmem_limit_bytes=LIMIT),
        cost_estimate=pl.CostEstimate(flops=micros * 10**9, bytes_accessed=0, transcendentals=0),
        name=name,
    )(*operands)


def load_kernel(*refs):
    count = len(refs) // 2
    copies = [pltpu.make_async_copy(refs[i], refs[count + i], refs[-1].at[i]) for i in range(count)]
    for copy in copies:
        copy.start()
    for copy in copies:
        copy.wait()


def load(*arrays):
    out = call(
        load_kernel,
        "load",
        [pltpu.VMEM(a.shape, a.dtype) for a in arrays],
        [HBM] * len(arrays),
        [pltpu.with_memory_space_constraint(a, pltpu.HBM) for a in arrays],
        scratch=[pltpu.SemaphoreType.DMA((len(arrays),))],
        micros=5,
    )
    return [pltpu.with_memory_space_constraint(a, pltpu.VMEM) for a in out]


def line_of(axis, rows):
    one, three, two = (from_wide(axis, bits, rows) for bits in (1, 3, 2))
    return [rows, one, two, three]


def assemble_kernel(first, early, place, *refs):
    parts, out = refs[:3], refs[3]
    z, x, y, c = place[0], place[1], place[2], place[3]
    block = out.shape[0] // 8
    for outer in (0, 1, 3) if early else (2,):
        for inner in range(4):
            dz, dx = (inner, outer) if first == "z" else (outer, inner)
            columns = pl.ds(pl.multiple_of(((z ^ dz) * 4 + (x ^ dx)) * LANES, LANES), LANES)
            if early:
                part, index = parts[(0, 1, None, 2)[outer]], inner
            else:
                part, index = parts[1 + inner // 2], inner % 2
            for side in range(2):
                core = 1 - c if side == 0 else c
                for j in range(4):
                    rows = pl.ds(pl.multiple_of(((y ^ j) * 2 + core) * block, block), block)
                    at = (side * 4 + j) * block
                    out[at : at + block, columns] = part[index, rows, :]


def assemble(first, place, parts, base=None):
    rows = parts[0].shape[1]
    operands = [place, *parts] if base is None else [place, base, *parts]
    return call(
        functools.partial(assemble_kernel, first, base is None),
        "assemble_" + first,
        jax.ShapeDtypeStruct((rows, 16 * LANES), BF16),
        [SMEM] + [VMEM] * (len(operands) - 1),
        operands,
        many=False,
        aliases={} if base is None else {1: 0},
    )


def project_other_kernel(rows, gate_weight, up_weight, out):
    units = gate_weight.shape[1]
    half = rows.shape[0] // 2
    for t in range(0, units, LANES):
        weights = jnp.concatenate([gate_weight[:, t : t + LANES], up_weight[:, t : t + LANES]], axis=1)
        term = jnp.dot(rows[:half, :], weights, preferred_element_type=F32)
        out[:, t : t + LANES] = term[:, :LANES]
        out[:, units + t : units + t + LANES] = term[:, LANES:]


def project_other(rows, gate_weight, up_weight):
    half = rows.shape[0] // 2
    units = gate_weight.shape[1]
    shape = jax.ShapeDtypeStruct((half, 2 * units), F32)
    return call(
        project_other_kernel, "project_other", shape, [VMEM] * 3, [rows, gate_weight, up_weight], micros=4, many=False
    )


def project_own_kernel(rows, gate_weight, up_weight, received, own, to_one, to_three, keep_one, keep_three):
    units = gate_weight.shape[1]
    half = rows.shape[0] // 2
    quarter = half // 4
    eighth = quarter // 2
    for t in range(0, units, LANES):
        weights = jnp.concatenate([gate_weight[:, t : t + LANES], up_weight[:, t : t + LANES]], axis=1)
        term = jnp.dot(rows[half:, :], weights, preferred_element_type=F32)
        for part in range(2):
            columns = slice(t + part * units, t + part * units + LANES)
            block = term[:, part * LANES : (part + 1) * LANES] + received[:, columns]
            at = lambda j, h: block[j * quarter + h * eighth : j * quarter + (h + 1) * eighth]
            own[:, columns] = block[:quarter]
            to_one[:eighth, columns] = at(2, 0).astype(BF16)
            to_one[eighth:, columns] = at(1, 0).astype(BF16)
            to_three[:eighth, columns] = at(2, 1).astype(BF16)
            to_three[eighth:, columns] = at(3, 1).astype(BF16)
            keep_one[:, columns] = at(1, 1)
            keep_three[:, columns] = at(3, 0)


def project_own(rows, gate_weight, up_weight, received):
    half = rows.shape[0] // 2
    units = gate_weight.shape[1]
    shapes = [
        jax.ShapeDtypeStruct((count, 2 * units), dtype)
        for count, dtype in ((half // 4, F32), (half // 4, BF16), (half // 4, BF16), (half // 8, F32), (half // 8, F32))
    ]
    return call(project_own_kernel, "project_own", shapes, [VMEM] * 4, [rows, gate_weight, up_weight, received], micros=4)


def relay_kernel(keep_one, keep_three, from_one, from_three, to_one, to_three):
    half = keep_one.shape[0]
    to_one[...] = (keep_one[...] + from_three[:half, :].astype(F32)).astype(BF16)
    to_three[...] = (keep_three[...] + from_one[:half, :].astype(F32)).astype(BF16)


def relay(parts, from_one, from_three):
    keeps = parts[3:]
    shape = jax.ShapeDtypeStruct(keeps[0].shape, BF16)
    return call(relay_kernel, "relay", [shape] * 2, [VMEM] * 4, [*keeps, from_one, from_three])


def sum_of(h, own, from_one, from_three, relay_one, relay_three):
    half = relay_one.shape[0]
    direct, relayed = (from_one, relay_three) if h == 0 else (from_three, relay_one)
    return own[h * half : (h + 1) * half, :] + direct[half:, :].astype(F32) + relayed[...].astype(F32)


def hidden_kernel(*refs):
    parts, out = refs[:-1], refs[-1]
    units = out.shape[1]
    half = out.shape[0] // 2
    for h in range(2):
        total = sum_of(h, *parts)
        gate, up = total[:, :units], total[:, units:]
        out[h * half : (h + 1) * half, :] = (gate / (1.0 + jnp.exp(-gate)) * up).astype(BF16)


def hidden_of(parts):
    rows, columns = parts[0].shape
    return call(
        hidden_kernel, "hidden", jax.ShapeDtypeStruct((rows, columns // 2), BF16), [VMEM] * 5, parts, many=False
    )


def down_kernel(first, place, rows, down_weight, own, to_one, to_three, keep_one, keep_three):
    z, x = place[0], place[1]
    half = rows.shape[0] // 2
    for outer in (2, 1, 3, 0):
        for pair in (0, 2):
            weights = []
            for inner in (pair, pair + 1):
                dz, dx = (outer, inner) if first == "z" else (inner, outer)
                column = ((z ^ dz) * 4 + (x ^ dx)) * LANES
                weights.append(down_weight[:, pl.ds(pl.multiple_of(column, LANES), LANES)])
            term = jnp.dot(rows[...], jnp.concatenate(weights, axis=1), preferred_element_type=F32)
            columns = slice(pair * LANES, (pair + 2) * LANES)
            if outer == 0:
                own[:, columns] = term
            elif outer == 1:
                to_one[half:, columns] = term[:half].astype(BF16)
                keep_one[:, columns] = term[half:]
            elif outer == 2:
                to_one[:half, columns] = term[:half].astype(BF16)
                to_three[:half, columns] = term[half:].astype(BF16)
            else:
                keep_three[:, columns] = term[:half]
                to_three[half:, columns] = term[half:].astype(BF16)


def down(first, place, rows, down_weight):
    count = rows.shape[0]
    width = down_weight.shape[1] // 4
    shapes = [
        jax.ShapeDtypeStruct((n, width), dtype)
        for n, dtype in ((count, F32), (count, BF16), (count, BF16), (count // 2, F32), (count // 2, F32))
    ]
    return call(
        functools.partial(down_kernel, first),
        "down_" + first,
        shapes,
        [SMEM, VMEM, VMEM],
        [place, rows, down_weight],
        micros=4,
    )


def add_kernel(own, from_one, from_three, relay_one, relay_three, *outs):
    half = relay_one.shape[0]
    for h in range(2):
        total = sum_of(h, own, from_one, from_three, relay_one, relay_three)
        for i, out in enumerate(outs):
            out[h * half : (h + 1) * half, :] = total[:, i * LANES : (i + 1) * LANES].astype(out.dtype)


def add_line(parts):
    shapes = [jax.ShapeDtypeStruct((parts[0].shape[0], LANES), F32 if j == 0 else BF16) for j in range(4)]
    return call(add_kernel, "add_line", shapes, [VMEM] * 5, parts)


def send(axis, parts):
    return [parts[0]] + [from_wide(axis, bits, parts[bits]) for bits in (1, 2, 3)]


def last_kernel(place, *refs):
    parts, out = refs[:-1], refs[-1]
    y, c = place[2], place[3]
    rows = parts[0].shape[0]
    block = rows // 8
    for chunk in range(2):
        total = parts[4 * chunk][...]
        for k in range(1, 4):
            total = total + parts[4 * chunk + k][...].astype(F32)
        total = total.astype(BF16)
        for side in range(2):
            core = c if side == 0 else 1 - c
            for j in range(4):
                at = chunk * rows + ((y ^ j) * 2 + core) * block
                value = total[(side * 4 + j) * block : (side * 4 + j + 1) * block]
                out[pl.ds(pl.multiple_of(at, block), block), :] = value


def last(place, parts):
    shape = jax.ShapeDtypeStruct((2 * parts[0].shape[0], LANES), BF16)
    return call(last_kernel, "last", shape, [SMEM] + [VMEM] * 8, [place, *parts], many=False)


def body(tokens, gate_weight, up_weight, down_weight):
    wide, narrow = lax.axis_index("wide"), lax.axis_index("narrow")
    place = jnp.stack([wide // 4, wide % 4, narrow // 2, narrow % 2]).astype(jnp.int32)
    rows = tokens.shape[0] // 2
    both = range(2)
    tokens = after(tokens, place)
    lines = [line_of(axis, tokens[at * rows : (at + 1) * rows]) for at, axis in enumerate("zx")]
    lines[0] = after(lines[0], lines[1][1])
    stacks = [jnp.stack(line) for line in lines]
    nexts = [[from_wide(axis, bits, stack) for bits in (1, 3)] for axis, stack in zip("xz", stacks)]
    *weights, down_weight = load(*after((gate_weight, up_weight, down_weight), stacks))
    nexts[0] = after(nexts[0], down_weight)
    bases = [assemble(axis, place, [stack, *near]) for axis, stack, near in zip("zx", stacks, nexts)]
    fars = [(from_wide(axis, 1, three[:2]), from_wide(axis, 3, one[2:])) for axis, (one, three) in zip("xz", nexts)]
    fars[0] = after(fars[0], bases[1])
    chunks = [assemble(axis, place, far, base) for axis, far, base in zip("zx", fars, bases)]
    others = []
    for at in both:
        others.append(project_other(after(chunks[at], *others), *weights))
    received = [swap(array) for array in others]
    parts = []
    for at in both:
        parts.append(project_own(after(chunks[at], others[1], *[p[0] for p in parts]), *weights, received[at]))
    def first_round(exchange, parts):
        return exchange(1, parts[1]), exchange(3, parts[2])

    def second_round(exchange, pair):
        return exchange(1, pair[0]), exchange(3, pair[1])

    together = lax.optimization_barrier
    half = parts[0][0].shape[0] // 2
    first = [first_round(from_y, p) for p in parts]
    second = [second_round(from_y, relay(parts[0], *after(first[0], parts[1][0]))), None]
    relayed = relay(parts[1], *first[1])
    second[0] = after(second[0], relayed[0])
    hidden = [hidden_of([parts[0][0], *first[0], *second[0]]), None]
    near = [[from_y(bits, hidden[0]) for bits in (1, 3)], None]
    second[1] = second_round(from_y, relayed)
    hidden[1] = hidden_of([parts[1][0], *first[1], *second[1]])
    near[1] = [from_y(bits, hidden[1]) for bits in (1, 3)]
    near[0] = after(near[0], hidden[1])
    far = [second_round(from_y, (near[0][1][:half], near[0][0][half:])), None]
    near[1], far[0] = together((near[1], far[0]))
    parts = []
    for at, axis in enumerate("zx"):
        if at == 1:
            far[1] = after(second_round(from_y, (near[1][1][:half], near[1][0][half:])), parts[0][0])
        rows_here = jnp.concatenate([hidden[at], near[at][0], *far[at], near[at][1]])
        parts.append(down(axis, place, jnp.concatenate([rows_here, swap(rows_here)]), down_weight))
    along = [functools.partial(from_wide, axis) for axis in "zx"]
    first = [first_round(exchange, p) for exchange, p in zip(along, parts)]
    second[0] = second_round(along[0], relay(parts[0], *after(first[0], parts[1][0])))
    relayed = relay(parts[1], *first[1])
    second[0] = after(second[0], relayed[0])
    second[1] = second_round(along[1], relayed)
    final = send("x", add_line([parts[0][0], *first[0], *second[0]]))
    second[1], final[1] = together((second[1], final[1]))
    return last(place, final + send("z", add_line([parts[1][0], *first[1], *second[1]])))


def solution(mesh):
    return jax.shard_map(
        body,
        mesh=mesh,
        in_specs=(
            P(None, ("narrow", "wide")),
            P("narrow", "wide"),
            P("narrow", "wide"),
            P("wide", "narrow"),
        ),
        out_specs=P(None, ("narrow", "wide")),
        check_vma=False,
    )
```

```python
import functools

import jax
import jax.numpy as jnp
from jax import lax
from jax.experimental import pallas as pl
from jax.experimental.pallas import tpu as pltpu
from jax.sharding import PartitionSpec as P

LANES = 128
LIMIT = 16 << 20
F32, BF16 = jnp.float32, jnp.bfloat16
VMEM = pl.BlockSpec(memory_space=pltpu.VMEM)
SMEM = pl.BlockSpec(memory_space=pltpu.SMEM)
HBM = pl.BlockSpec(memory_space=pltpu.HBM)


def from_wide(axis, bits, array):
    step = bits * 4 if axis == "z" else bits
    return lax.ppermute(array, "wide", [(i ^ step, i) for i in range(16)])


def from_y(bits, array):
    return lax.ppermute(array, "narrow", [(i ^ (bits * 2), i) for i in range(8)])


def swap(array):
    return lax.ppermute(array, "narrow", [(i ^ 1, i) for i in range(8)])


def after(value, *earlier):
    return lax.optimization_barrier((value, *earlier))[0]


def call(kernel, name, out_shape, in_specs, operands, scratch=(), micros=0, many=True, aliases={}):
    return pl.pallas_call(
        kernel,
        out_shape=out_shape,
        in_specs=in_specs,
        out_specs=[VMEM] * len(out_shape) if many else VMEM,
        scratch_shapes=scratch,
        input_output_aliases=aliases,
        compiler_params=pltpu.CompilerParams(vmem_limit_bytes=LIMIT),
        cost_estimate=pl.CostEstimate(flops=micros * 10**9, bytes_accessed=0, transcendentals=0),
        name=name,
    )(*operands)


def load_kernel(place, gate_hbm, up_hbm, down_hbm, gate, up, down, sem):
    z, x = place[0], place[1]
    copies = [pltpu.make_async_copy(gate_hbm, gate, sem.at[0]), pltpu.make_async_copy(up_hbm, up, sem.at[1])]
    for dz in range(4):
        for dx in range(4):
            at = dz * 4 + dx
            source = pl.ds(pl.multiple_of(((z ^ dz) * 4 + (x ^ dx)) * LANES, LANES), LANES)
            target = slice(at * LANES, (at + 1) * LANES)
            copies.append(pltpu.make_async_copy(down_hbm.at[:, source], down.at[:, target], sem.at[2 + at]))
    for copy in copies:
        copy.start()
    for copy in copies:
        copy.wait()


def load(place, *weights):
    out = call(
        load_kernel,
        "load",
        [pltpu.VMEM(w.shape, w.dtype) for w in weights],
        [SMEM] + [HBM] * 3,
        [place] + [pltpu.with_memory_space_constraint(w, pltpu.HBM) for w in weights],
        scratch=[pltpu.SemaphoreType.DMA((18,))],
        micros=5,
    )
    return [pltpu.with_memory_space_constraint(w, pltpu.VMEM) for w in out]


def line_of(axis, rows):
    one, three, two = (from_wide(axis, bits, rows) for bits in (1, 3, 2))
    return [rows, one, two, three]


def assemble_kernel(first, early, place, *refs):
    parts, out = refs[:3], refs[3]
    z, x, y, c = place[0], place[1], place[2], place[3]
    block = out.shape[0] // 8
    for outer in (0, 1, 3) if early else (2,):
        for inner in range(4):
            dz, dx = (inner, outer) if first == "z" else (outer, inner)
            columns = pl.ds(pl.multiple_of(((z ^ dz) * 4 + (x ^ dx)) * LANES, LANES), LANES)
            if early:
                part, index = parts[(0, 1, None, 2)[outer]], inner
            else:
                part, index = parts[1 + inner // 2], inner % 2
            for side in range(2):
                core = 1 - c if side == 0 else c
                for j in range(4):
                    rows = pl.ds(pl.multiple_of(((y ^ j) * 2 + core) * block, block), block)
                    at = (side * 4 + j) * block
                    out[at : at + block, columns] = part[index, rows, :]


def assemble(first, place, parts, base=None):
    rows = parts[0].shape[1]
    operands = [place, *parts] if base is None else [place, base, *parts]
    return call(
        functools.partial(assemble_kernel, first, base is None),
        "assemble_" + first,
        jax.ShapeDtypeStruct((rows, 16 * LANES), BF16),
        [SMEM] + [VMEM] * (len(operands) - 1),
        operands,
        many=False,
        aliases={} if base is None else {1: 0},
    )


def project_other_kernel(rows, gate_weight, up_weight, out):
    units = gate_weight.shape[1]
    half = rows.shape[0] // 2
    for t in range(0, units, LANES):
        weights = jnp.concatenate([gate_weight[:, t : t + LANES], up_weight[:, t : t + LANES]], axis=1)
        term = jnp.dot(rows[:half, :], weights, preferred_element_type=F32)
        out[:, t : t + LANES] = term[:, :LANES]
        out[:, units + t : units + t + LANES] = term[:, LANES:]


def project_other(rows, gate_weight, up_weight):
    half = rows.shape[0] // 2
    units = gate_weight.shape[1]
    shape = jax.ShapeDtypeStruct((half, 2 * units), F32)
    return call(
        project_other_kernel, "project_other", shape, [VMEM] * 3, [rows, gate_weight, up_weight], micros=4, many=False
    )


def project_own_kernel(rows, gate_weight, up_weight, received, own, to_one, to_three, keep_one, keep_three):
    units = gate_weight.shape[1]
    half = rows.shape[0] // 2
    quarter = half // 4
    eighth = quarter // 2
    for t in range(0, units, LANES):
        weights = jnp.concatenate([gate_weight[:, t : t + LANES], up_weight[:, t : t + LANES]], axis=1)
        term = jnp.dot(rows[half:, :], weights, preferred_element_type=F32)
        for part in range(2):
            columns = slice(t + part * units, t + part * units + LANES)
            block = term[:, part * LANES : (part + 1) * LANES] + received[:, columns]
            at = lambda j, h: block[j * quarter + h * eighth : j * quarter + (h + 1) * eighth]
            own[:, columns] = block[:quarter]
            to_one[:eighth, columns] = at(2, 0).astype(BF16)
            to_one[eighth:, columns] = at(1, 0).astype(BF16)
            to_three[:eighth, columns] = at(2, 1).astype(BF16)
            to_three[eighth:, columns] = at(3, 1).astype(BF16)
            keep_one[:, columns] = at(1, 1)
            keep_three[:, columns] = at(3, 0)


def project_own(rows, gate_weight, up_weight, received):
    half = rows.shape[0] // 2
    units = gate_weight.shape[1]
    shapes = [
        jax.ShapeDtypeStruct((count, 2 * units), dtype)
        for count, dtype in ((half // 4, F32), (half // 4, BF16), (half // 4, BF16), (half // 8, F32), (half // 8, F32))
    ]
    return call(project_own_kernel, "project_own", shapes, [VMEM] * 4, [rows, gate_weight, up_weight, received], micros=4)


def relay_kernel(keep_one, keep_three, from_one, from_three, to_one, to_three):
    half = keep_one.shape[0]
    to_one[...] = (keep_one[...] + from_three[:half, :].astype(F32)).astype(BF16)
    to_three[...] = (keep_three[...] + from_one[:half, :].astype(F32)).astype(BF16)


def relay(parts, from_one, from_three):
    keeps = parts[3:]
    shape = jax.ShapeDtypeStruct(keeps[0].shape, BF16)
    return call(relay_kernel, "relay", [shape] * 2, [VMEM] * 4, [*keeps, from_one, from_three])


def sum_of(h, own, from_one, from_three, relay_one, relay_three):
    half = relay_one.shape[0]
    direct, relayed = (from_one, relay_three) if h == 0 else (from_three, relay_one)
    return own[h * half : (h + 1) * half, :] + direct[half:, :].astype(F32) + relayed[...].astype(F32)


def hidden_kernel(*refs):
    parts, out = refs[:-1], refs[-1]
    units = out.shape[1]
    half = out.shape[0] // 2
    for h in range(2):
        total = sum_of(h, *parts)
        gate, up = total[:, :units], total[:, units:]
        out[h * half : (h + 1) * half, :] = (gate / (1.0 + jnp.exp(-gate)) * up).astype(BF16)


def hidden_of(parts):
    rows, columns = parts[0].shape
    return call(
        hidden_kernel, "hidden", jax.ShapeDtypeStruct((rows, columns // 2), BF16), [VMEM] * 5, parts, many=False
    )


def down_kernel(first, rows, down_weight, own, to_one, to_three, keep_one, keep_three):
    half = rows.shape[0] // 2
    for outer in (2, 1, 3, 0):
        for pair in (0, 2):
            if first == "z":
                at = outer * 4 + pair
                weights = down_weight[:, at * LANES : (at + 2) * LANES]
            else:
                blocks = [pair * 4 + outer, (pair + 1) * 4 + outer]
                weights = jnp.concatenate([down_weight[:, at * LANES : (at + 1) * LANES] for at in blocks], axis=1)
            term = jnp.dot(rows[...], weights, preferred_element_type=F32)
            columns = slice(pair * LANES, (pair + 2) * LANES)
            if outer == 0:
                own[:, columns] = term
            elif outer == 1:
                to_one[half:, columns] = term[:half].astype(BF16)
                keep_one[:, columns] = term[half:]
            elif outer == 2:
                to_one[:half, columns] = term[:half].astype(BF16)
                to_three[:half, columns] = term[half:].astype(BF16)
            else:
                keep_three[:, columns] = term[:half]
                to_three[half:, columns] = term[half:].astype(BF16)


def down(first, rows, down_weight):
    count = rows.shape[0]
    width = down_weight.shape[1] // 4
    shapes = [
        jax.ShapeDtypeStruct((n, width), dtype)
        for n, dtype in ((count, F32), (count, BF16), (count, BF16), (count // 2, F32), (count // 2, F32))
    ]
    return call(
        functools.partial(down_kernel, first),
        "down_" + first,
        shapes,
        [VMEM, VMEM],
        [rows, down_weight],
        micros=4,
    )


def add_kernel(own, from_one, from_three, relay_one, relay_three, *outs):
    half = relay_one.shape[0]
    for h in range(2):
        total = sum_of(h, own, from_one, from_three, relay_one, relay_three)
        for i, out in enumerate(outs):
            out[h * half : (h + 1) * half, :] = total[:, i * LANES : (i + 1) * LANES].astype(out.dtype)


def add_line(parts):
    shapes = [jax.ShapeDtypeStruct((parts[0].shape[0], LANES), F32 if j == 0 else BF16) for j in range(4)]
    return call(add_kernel, "add_line", shapes, [VMEM] * 5, parts)


def send(axis, parts):
    return [parts[0]] + [from_wide(axis, bits, parts[bits]) for bits in (1, 2, 3)]


def last_kernel(place, *refs):
    parts, out = refs[:-1], refs[-1]
    y, c = place[2], place[3]
    rows = parts[0].shape[0]
    block = rows // 8
    for chunk in range(2):
        total = parts[4 * chunk][...]
        for k in range(1, 4):
            total = total + parts[4 * chunk + k][...].astype(F32)
        total = total.astype(BF16)
        for side in range(2):
            core = c if side == 0 else 1 - c
            for j in range(4):
                at = chunk * rows + ((y ^ j) * 2 + core) * block
                value = total[(side * 4 + j) * block : (side * 4 + j + 1) * block]
                out[pl.ds(pl.multiple_of(at, block), block), :] = value


def last(place, parts):
    shape = jax.ShapeDtypeStruct((2 * parts[0].shape[0], LANES), BF16)
    return call(last_kernel, "last", shape, [SMEM] + [VMEM] * 8, [place, *parts], many=False)


def body(tokens, gate_weight, up_weight, down_weight):
    wide, narrow = lax.axis_index("wide"), lax.axis_index("narrow")
    place = jnp.stack([wide // 4, wide % 4, narrow // 2, narrow % 2]).astype(jnp.int32)
    rows = tokens.shape[0] // 2
    both = range(2)
    tokens = after(tokens, place)
    lines = [line_of(axis, tokens[at * rows : (at + 1) * rows]) for at, axis in enumerate("zx")]
    lines[0] = after(lines[0], lines[1][1])
    stacks = [jnp.stack(line) for line in lines]
    nexts = [[from_wide(axis, bits, stack) for bits in (1, 3)] for axis, stack in zip("xz", stacks)]
    *weights, down_weight = load(place, *after((gate_weight, up_weight, down_weight), stacks))
    nexts[0] = after(nexts[0], down_weight)
    bases = [assemble(axis, place, [stack, *near]) for axis, stack, near in zip("zx", stacks, nexts)]
    fars = [(from_wide(axis, 1, three[:2]), from_wide(axis, 3, one[2:])) for axis, (one, three) in zip("xz", nexts)]
    fars[0] = after(fars[0], bases[1])
    chunks = [assemble(axis, place, far, base) for axis, far, base in zip("zx", fars, bases)]
    others = []
    for at in both:
        others.append(project_other(after(chunks[at], *others), *weights))
    received = [swap(array) for array in others]
    parts = []
    for at in both:
        parts.append(project_own(after(chunks[at], others[1], *[p[0] for p in parts]), *weights, received[at]))
    def first_round(exchange, parts):
        return exchange(1, parts[1]), exchange(3, parts[2])

    def second_round(exchange, pair):
        return exchange(1, pair[0]), exchange(3, pair[1])

    together = lax.optimization_barrier
    half = parts[0][0].shape[0] // 2
    first = [first_round(from_y, p) for p in parts]
    second = [second_round(from_y, relay(parts[0], *after(first[0], parts[1][0]))), None]
    relayed = relay(parts[1], *first[1])
    second[0] = after(second[0], relayed[0])
    hidden = [hidden_of([parts[0][0], *first[0], *second[0]]), None]
    near = [[from_y(bits, hidden[0]) for bits in (1, 3)], None]
    second[1] = second_round(from_y, relayed)
    hidden[1] = hidden_of([parts[1][0], *first[1], *second[1]])
    near[1] = [from_y(bits, hidden[1]) for bits in (1, 3)]
    near[0] = after(near[0], hidden[1])
    far = [second_round(from_y, (near[0][1][:half], near[0][0][half:])), None]
    near[1], far[0] = together((near[1], far[0]))
    parts = []
    for at, axis in enumerate("zx"):
        if at == 1:
            far[1] = after(second_round(from_y, (near[1][1][:half], near[1][0][half:])), parts[0][0])
        rows_here = jnp.concatenate([hidden[at], near[at][0], *far[at], near[at][1]])
        parts.append(down(axis, jnp.concatenate([rows_here, swap(rows_here)]), down_weight))
    along = [functools.partial(from_wide, axis) for axis in "zx"]
    first = [first_round(exchange, p) for exchange, p in zip(along, parts)]
    second[0] = second_round(along[0], relay(parts[0], *after(first[0], parts[1][0])))
    relayed = relay(parts[1], *first[1])
    second[0] = after(second[0], relayed[0])
    second[1] = second_round(along[1], relayed)
    final = send("x", add_line([parts[0][0], *first[0], *second[0]]))
    second[1] = after(second[1], relayed[0])
    return last(place, final + send("z", add_line([parts[1][0], *first[1], *second[1]])))


def solution(mesh):
    return jax.shard_map(
        body,
        mesh=mesh,
        in_specs=(
            P(None, ("narrow", "wide")),
            P("narrow", "wide"),
            P("narrow", "wide"),
            P("wide", "narrow"),
        ),
        out_specs=P(None, ("narrow", "wide")),
        check_vma=False,
    )
```

```python
import functools

import jax
import jax.numpy as jnp
from jax import lax
from jax.experimental import pallas as pl
from jax.experimental.pallas import tpu as pltpu
from jax.sharding import PartitionSpec as P

LANES = 128
LIMIT = 16 << 20
F32, BF16 = jnp.float32, jnp.bfloat16
VMEM = pl.BlockSpec(memory_space=pltpu.VMEM)
SMEM = pl.BlockSpec(memory_space=pltpu.SMEM)
HBM = pl.BlockSpec(memory_space=pltpu.HBM)


def from_wide(axis, bits, array):
    step = bits * 4 if axis == "z" else bits
    return lax.ppermute(array, "wide", [(i ^ step, i) for i in range(16)])


def from_y(bits, array):
    return lax.ppermute(array, "narrow", [(i ^ (bits * 2), i) for i in range(8)])


def swap(array):
    return lax.ppermute(array, "narrow", [(i ^ 1, i) for i in range(8)])


def after(value, *earlier):
    return lax.optimization_barrier((value, *earlier))[0]


def call(kernel, name, out_shape, in_specs, operands, scratch=(), micros=0, many=True, aliases={}):
    return pl.pallas_call(
        kernel,
        out_shape=out_shape,
        in_specs=in_specs,
        out_specs=[VMEM] * len(out_shape) if many else VMEM,
        scratch_shapes=scratch,
        input_output_aliases=aliases,
        compiler_params=pltpu.CompilerParams(vmem_limit_bytes=LIMIT),
        cost_estimate=pl.CostEstimate(flops=micros * 10**9, bytes_accessed=0, transcendentals=0),
        name=name,
    )(*operands)


def load_kernel(place, gate_hbm, up_hbm, down_hbm, gate, up, down, sem):
    z, x = place[0], place[1]
    copies = [pltpu.make_async_copy(gate_hbm, gate, sem.at[0]), pltpu.make_async_copy(up_hbm, up, sem.at[1])]
    for dz in range(4):
        for dx in range(4):
            at = dz * 4 + dx
            source = pl.ds(pl.multiple_of(((z ^ dz) * 4 + (x ^ dx)) * LANES, LANES), LANES)
            target = slice(at * LANES, (at + 1) * LANES)
            copies.append(pltpu.make_async_copy(down_hbm.at[:, source], down.at[:, target], sem.at[2 + at]))
    for copy in copies:
        copy.start()
    for copy in copies:
        copy.wait()


def load(place, *weights):
    out = call(
        load_kernel,
        "load",
        [pltpu.VMEM(w.shape, w.dtype) for w in weights],
        [SMEM] + [HBM] * 3,
        [place] + [pltpu.with_memory_space_constraint(w, pltpu.HBM) for w in weights],
        scratch=[pltpu.SemaphoreType.DMA((18,))],
        micros=5,
    )
    return [pltpu.with_memory_space_constraint(w, pltpu.VMEM) for w in out]


def line_of(axis, rows):
    one, three, two = (from_wide(axis, bits, rows) for bits in (1, 3, 2))
    return [rows, one, two, three]


def assemble_kernel(first, early, place, *refs):
    parts, out = refs[:3], refs[3]
    z, x, y, c = place[0], place[1], place[2], place[3]
    block = out.shape[0] // 8
    for outer in (0, 1, 3) if early else (2,):
        for inner in range(4):
            dz, dx = (inner, outer) if first == "z" else (outer, inner)
            columns = pl.ds(pl.multiple_of(((z ^ dz) * 4 + (x ^ dx)) * LANES, LANES), LANES)
            if early:
                part, index = parts[(0, 1, None, 2)[outer]], inner
            else:
                part, index = parts[1 + inner // 2], inner % 2
            for side in range(2):
                core = 1 - c if side == 0 else c
                for j in range(4):
                    rows = pl.ds(pl.multiple_of(((y ^ j) * 2 + core) * block, block), block)
                    at = (side * 4 + j) * block
                    out[at : at + block, columns] = part[index, rows, :]


def assemble(first, place, parts, base=None):
    rows = parts[0].shape[1]
    operands = [place, *parts] if base is None else [place, base, *parts]
    return call(
        functools.partial(assemble_kernel, first, base is None),
        "assemble_" + first,
        jax.ShapeDtypeStruct((rows, 16 * LANES), BF16),
        [SMEM] + [VMEM] * (len(operands) - 1),
        operands,
        many=False,
        aliases={} if base is None else {1: 0},
    )


def pairs_of(units):
    return [(t, min(2 * LANES, units - t)) for t in range(0, units, 2 * LANES)]


def project_other_kernel(rows, gate_weight, up_weight, out):
    units = gate_weight.shape[1]
    half = rows.shape[0] // 2
    for t, width in pairs_of(units):
        weights = jnp.concatenate([gate_weight[:, t : t + width], up_weight[:, t : t + width]], axis=1)
        term = jnp.dot(rows[:half, :], weights, preferred_element_type=F32)
        out[:, t : t + width] = term[:, :width]
        out[:, units + t : units + t + width] = term[:, width:]


def project_other(rows, gate_weight, up_weight):
    half = rows.shape[0] // 2
    units = gate_weight.shape[1]
    shape = jax.ShapeDtypeStruct((half, 2 * units), F32)
    return call(
        project_other_kernel, "project_other", shape, [VMEM] * 3, [rows, gate_weight, up_weight], micros=4, many=False
    )


def project_own_kernel(rows, gate_weight, up_weight, received, own, to_one, to_three, keep_one, keep_three):
    units = gate_weight.shape[1]
    half = rows.shape[0] // 2
    quarter = half // 4
    eighth = quarter // 2
    for t, width in pairs_of(units):
        weights = jnp.concatenate([gate_weight[:, t : t + width], up_weight[:, t : t + width]], axis=1)
        term = jnp.dot(rows[half:, :], weights, preferred_element_type=F32)
        for part in range(2):
            columns = slice(t + part * units, t + part * units + width)
            block = term[:, part * width : (part + 1) * width] + received[:, columns]
            at = lambda j, h: block[j * quarter + h * eighth : j * quarter + (h + 1) * eighth]
            own[:, columns] = block[:quarter]
            to_one[:eighth, columns] = at(2, 0).astype(BF16)
            to_one[eighth:, columns] = at(1, 0).astype(BF16)
            to_three[:eighth, columns] = at(2, 1).astype(BF16)
            to_three[eighth:, columns] = at(3, 1).astype(BF16)
            keep_one[:, columns] = at(1, 1)
            keep_three[:, columns] = at(3, 0)


def project_own(rows, gate_weight, up_weight, received):
    half = rows.shape[0] // 2
    units = gate_weight.shape[1]
    shapes = [
        jax.ShapeDtypeStruct((count, 2 * units), dtype)
        for count, dtype in ((half // 4, F32), (half // 4, BF16), (half // 4, BF16), (half // 8, F32), (half // 8, F32))
    ]
    return call(project_own_kernel, "project_own", shapes, [VMEM] * 4, [rows, gate_weight, up_weight, received], micros=4)


def relay_kernel(keep_one, keep_three, from_one, from_three, to_one, to_three):
    half = keep_one.shape[0]
    to_one[...] = (keep_one[...] + from_three[:half, :].astype(F32)).astype(BF16)
    to_three[...] = (keep_three[...] + from_one[:half, :].astype(F32)).astype(BF16)


def relay(parts, from_one, from_three):
    keeps = parts[3:]
    shape = jax.ShapeDtypeStruct(keeps[0].shape, BF16)
    return call(relay_kernel, "relay", [shape] * 2, [VMEM] * 4, [*keeps, from_one, from_three])


def sum_of(h, own, from_one, from_three, relay_one, relay_three):
    half = relay_one.shape[0]
    direct, relayed = (from_one, relay_three) if h == 0 else (from_three, relay_one)
    return own[h * half : (h + 1) * half, :] + direct[half:, :].astype(F32) + relayed[...].astype(F32)


def hidden_kernel(*refs):
    parts, out = refs[:-1], refs[-1]
    units = out.shape[1]
    half = out.shape[0] // 2
    for h in range(2):
        total = sum_of(h, *parts)
        gate, up = total[:, :units], total[:, units:]
        out[h * half : (h + 1) * half, :] = (gate / (1.0 + jnp.exp(-gate)) * up).astype(BF16)


def hidden_of(parts):
    rows, columns = parts[0].shape
    return call(
        hidden_kernel, "hidden", jax.ShapeDtypeStruct((rows, columns // 2), BF16), [VMEM] * 5, parts, many=False
    )


def down_kernel(first, rows, down_weight, own, to_one, to_three, keep_one, keep_three):
    half = rows.shape[0] // 2
    for outer in (2, 1, 3, 0):
        for pair in (0, 2):
            if first == "z":
                at = outer * 4 + pair
                weights = down_weight[:, at * LANES : (at + 2) * LANES]
            else:
                blocks = [pair * 4 + outer, (pair + 1) * 4 + outer]
                weights = jnp.concatenate([down_weight[:, at * LANES : (at + 1) * LANES] for at in blocks], axis=1)
            term = jnp.dot(rows[...], weights, preferred_element_type=F32)
            columns = slice(pair * LANES, (pair + 2) * LANES)
            if outer == 0:
                own[:, columns] = term
            elif outer == 1:
                to_one[half:, columns] = term[:half].astype(BF16)
                keep_one[:, columns] = term[half:]
            elif outer == 2:
                to_one[:half, columns] = term[:half].astype(BF16)
                to_three[:half, columns] = term[half:].astype(BF16)
            else:
                keep_three[:, columns] = term[:half]
                to_three[half:, columns] = term[half:].astype(BF16)


def down(first, rows, down_weight):
    count = rows.shape[0]
    width = down_weight.shape[1] // 4
    shapes = [
        jax.ShapeDtypeStruct((n, width), dtype)
        for n, dtype in ((count, F32), (count, BF16), (count, BF16), (count // 2, F32), (count // 2, F32))
    ]
    return call(
        functools.partial(down_kernel, first),
        "down_" + first,
        shapes,
        [VMEM, VMEM],
        [rows, down_weight],
        micros=4,
    )


def add_kernel(own, from_one, from_three, relay_one, relay_three, *outs):
    half = relay_one.shape[0]
    for h in range(2):
        total = sum_of(h, own, from_one, from_three, relay_one, relay_three)
        for i, out in enumerate(outs):
            out[h * half : (h + 1) * half, :] = total[:, i * LANES : (i + 1) * LANES].astype(out.dtype)


def add_line(parts):
    shapes = [jax.ShapeDtypeStruct((parts[0].shape[0], LANES), F32 if j == 0 else BF16) for j in range(4)]
    return call(add_kernel, "add_line", shapes, [VMEM] * 5, parts)


def send(axis, parts):
    return [parts[0]] + [from_wide(axis, bits, parts[bits]) for bits in (1, 2, 3)]


def last_kernel(place, *refs):
    parts, out = refs[:-1], refs[-1]
    y, c = place[2], place[3]
    rows = parts[0].shape[0]
    block = rows // 8
    for chunk in range(2):
        total = parts[4 * chunk][...]
        for k in range(1, 4):
            total = total + parts[4 * chunk + k][...].astype(F32)
        total = total.astype(BF16)
        for side in range(2):
            core = c if side == 0 else 1 - c
            for j in range(4):
                at = chunk * rows + ((y ^ j) * 2 + core) * block
                value = total[(side * 4 + j) * block : (side * 4 + j + 1) * block]
                out[pl.ds(pl.multiple_of(at, block), block), :] = value


def last(place, parts):
    shape = jax.ShapeDtypeStruct((2 * parts[0].shape[0], LANES), BF16)
    return call(last_kernel, "last", shape, [SMEM] + [VMEM] * 8, [place, *parts], many=False)


def body(tokens, gate_weight, up_weight, down_weight):
    wide, narrow = lax.axis_index("wide"), lax.axis_index("narrow")
    place = jnp.stack([wide // 4, wide % 4, narrow // 2, narrow % 2]).astype(jnp.int32)
    rows = tokens.shape[0] // 2
    both = range(2)
    tokens = after(tokens, place)
    lines = [line_of(axis, tokens[at * rows : (at + 1) * rows]) for at, axis in enumerate("zx")]
    lines[0] = after(lines[0], lines[1][1])
    stacks = [jnp.stack(line) for line in lines]
    nexts = [[from_wide(axis, bits, stack) for bits in (1, 3)] for axis, stack in zip("xz", stacks)]
    *weights, down_weight = load(place, *after((gate_weight, up_weight, down_weight), stacks))
    nexts[0] = after(nexts[0], down_weight)
    bases = [assemble(axis, place, [stack, *near]) for axis, stack, near in zip("zx", stacks, nexts)]
    fars = [(from_wide(axis, 1, three[:2]), from_wide(axis, 3, one[2:])) for axis, (one, three) in zip("xz", nexts)]
    fars[0] = after(fars[0], bases[1])
    chunks = [assemble(axis, place, far, base) for axis, far, base in zip("zx", fars, bases)]
    others = []
    for at in both:
        others.append(project_other(after(chunks[at], *others), *weights))
    received = [swap(array) for array in others]
    parts = []
    for at in both:
        parts.append(project_own(after(chunks[at], others[1], *[p[0] for p in parts]), *weights, received[at]))
    def first_round(exchange, parts):
        return exchange(1, parts[1]), exchange(3, parts[2])

    def second_round(exchange, pair):
        return exchange(1, pair[0]), exchange(3, pair[1])

    together = lax.optimization_barrier
    half = parts[0][0].shape[0] // 2
    first = [first_round(from_y, p) for p in parts]
    second = [second_round(from_y, relay(parts[0], *after(first[0], parts[1][0]))), None]
    relayed = relay(parts[1], *first[1])
    second[0] = after(second[0], relayed[0])
    hidden = [hidden_of([parts[0][0], *first[0], *second[0]]), None]
    near = [[from_y(bits, hidden[0]) for bits in (1, 3)], None]
    second[1] = second_round(from_y, relayed)
    hidden[1] = hidden_of([parts[1][0], *first[1], *second[1]])
    near[1] = [from_y(bits, hidden[1]) for bits in (1, 3)]
    near[0] = after(near[0], hidden[1])
    far = [second_round(from_y, (near[0][1][:half], near[0][0][half:])), None]
    near[1], far[0] = together((near[1], far[0]))
    parts = []
    for at, axis in enumerate("zx"):
        if at == 1:
            far[1] = after(second_round(from_y, (near[1][1][:half], near[1][0][half:])), parts[0][0])
        rows_here = jnp.concatenate([hidden[at], near[at][0], *far[at], near[at][1]])
        parts.append(down(axis, jnp.concatenate([rows_here, swap(rows_here)]), down_weight))
    along = [functools.partial(from_wide, axis) for axis in "zx"]
    first = [first_round(exchange, p) for exchange, p in zip(along, parts)]
    second[0] = second_round(along[0], relay(parts[0], *after(first[0], parts[1][0])))
    relayed = relay(parts[1], *first[1])
    second[1] = second_round(along[1], relayed)
    final = send("x", add_line([parts[0][0], *first[0], *second[0]]))
    return last(place, final + send("z", add_line([parts[1][0], *first[1], *second[1]])))


def solution(mesh):
    return jax.shard_map(
        body,
        mesh=mesh,
        in_specs=(
            P(None, ("narrow", "wide")),
            P("narrow", "wide"),
            P("narrow", "wide"),
            P("wide", "narrow"),
        ),
        out_specs=P(None, ("narrow", "wide")),
        check_vma=False,
    )
```

```python
import functools

import jax
import jax.numpy as jnp
from jax import lax
from jax.experimental import pallas as pl
from jax.experimental.pallas import tpu as pltpu
from jax.sharding import PartitionSpec as P

LANES = 128
LIMIT = 16 << 20
F32, BF16 = jnp.float32, jnp.bfloat16
VMEM = pl.BlockSpec(memory_space=pltpu.VMEM)
SMEM = pl.BlockSpec(memory_space=pltpu.SMEM)
HBM = pl.BlockSpec(memory_space=pltpu.HBM)


def from_wide(axis, bits, array):
    step = bits * 4 if axis == "z" else bits
    return lax.ppermute(array, "wide", [(i ^ step, i) for i in range(16)])


def from_y(bits, array):
    return lax.ppermute(array, "narrow", [(i ^ (bits * 2), i) for i in range(8)])


def swap(array):
    return lax.ppermute(array, "narrow", [(i ^ 1, i) for i in range(8)])


def after(value, *earlier):
    return lax.optimization_barrier((value, *earlier))[0]


def call(kernel, name, out_shape, in_specs, operands, scratch=(), micros=0, many=True, aliases={}):
    return pl.pallas_call(
        kernel,
        out_shape=out_shape,
        in_specs=in_specs,
        out_specs=[VMEM] * len(out_shape) if many else VMEM,
        scratch_shapes=scratch,
        input_output_aliases=aliases,
        compiler_params=pltpu.CompilerParams(vmem_limit_bytes=LIMIT),
        cost_estimate=pl.CostEstimate(flops=micros * 10**9, bytes_accessed=0, transcendentals=0),
        name=name,
    )(*operands)


def load_kernel(permuted, place, *refs):
    count = (len(refs) - 1) // 2
    sem = refs[-1]
    z, x = place[0], place[1]
    copies = []
    if permuted:
        for at in range(16):
            source = pl.ds(pl.multiple_of(((z ^ (at // 4)) * 4 + (x ^ (at % 4))) * LANES, LANES), LANES)
            target = slice(at * LANES, (at + 1) * LANES)
            copies.append(pltpu.make_async_copy(refs[0].at[:, source], refs[1].at[:, target], sem.at[at]))
    else:
        copies = [pltpu.make_async_copy(refs[i], refs[count + i], sem.at[i]) for i in range(count)]
    for copy in copies:
        copy.start()
    for copy in copies:
        copy.wait()


def load(permuted, place, *weights):
    out = call(
        functools.partial(load_kernel, permuted),
        "load",
        [pltpu.VMEM(w.shape, w.dtype) for w in weights],
        [SMEM] + [HBM] * len(weights),
        [place] + [pltpu.with_memory_space_constraint(w, pltpu.HBM) for w in weights],
        scratch=[pltpu.SemaphoreType.DMA((16,))],
        micros=4,
    )
    return [pltpu.with_memory_space_constraint(w, pltpu.VMEM) for w in out]


def line_of(axis, rows):
    one, three, two = (from_wide(axis, bits, rows) for bits in (1, 3, 2))
    return [rows, one, two, three]


def assemble_kernel(first, early, place, *refs):
    parts, out = refs[:3], refs[3]
    z, x, y, c = place[0], place[1], place[2], place[3]
    block = out.shape[0] // 8
    for outer in (0, 1, 3) if early else (2,):
        for inner in range(4):
            dz, dx = (inner, outer) if first == "z" else (outer, inner)
            columns = pl.ds(pl.multiple_of(((z ^ dz) * 4 + (x ^ dx)) * LANES, LANES), LANES)
            if early:
                part, index = parts[(0, 1, None, 2)[outer]], inner
            else:
                part, index = parts[1 + inner // 2], inner % 2
            for side in range(2):
                core = 1 - c if side == 0 else c
                for j in range(4):
                    rows = pl.ds(pl.multiple_of(((y ^ j) * 2 + core) * block, block), block)
                    at = (side * 4 + j) * block
                    out[at : at + block, columns] = part[index, rows, :]


def assemble(first, place, parts, base=None):
    rows = parts[0].shape[1]
    operands = [place, *parts] if base is None else [place, base, *parts]
    return call(
        functools.partial(assemble_kernel, first, base is None),
        "assemble_" + first,
        jax.ShapeDtypeStruct((rows, 16 * LANES), BF16),
        [SMEM] + [VMEM] * (len(operands) - 1),
        operands,
        many=False,
        aliases={} if base is None else {1: 0},
    )


def pairs_of(units):
    return [(t, min(2 * LANES, units - t)) for t in range(0, units, 2 * LANES)]


def project_other_kernel(rows, gate_weight, up_weight, out):
    units = gate_weight.shape[1]
    half = rows.shape[0] // 2
    for t, width in pairs_of(units):
        weights = jnp.concatenate([gate_weight[:, t : t + width], up_weight[:, t : t + width]], axis=1)
        term = jnp.dot(rows[:half, :], weights, preferred_element_type=F32)
        out[:, t : t + width] = term[:, :width]
        out[:, units + t : units + t + width] = term[:, width:]


def project_other(rows, gate_weight, up_weight):
    half = rows.shape[0] // 2
    units = gate_weight.shape[1]
    shape = jax.ShapeDtypeStruct((half, 2 * units), F32)
    return call(
        project_other_kernel, "project_other", shape, [VMEM] * 3, [rows, gate_weight, up_weight], micros=4, many=False
    )


def project_own_kernel(rows, gate_weight, up_weight, received, own, to_one, to_three, keep_one, keep_three):
    units = gate_weight.shape[1]
    half = rows.shape[0] // 2
    quarter = half // 4
    eighth = quarter // 2
    for t, width in pairs_of(units):
        weights = jnp.concatenate([gate_weight[:, t : t + width], up_weight[:, t : t + width]], axis=1)
        term = jnp.dot(rows[half:, :], weights, preferred_element_type=F32)
        for part in range(2):
            columns = slice(t + part * units, t + part * units + width)
            block = term[:, part * width : (part + 1) * width] + received[:, columns]
            at = lambda j, h: block[j * quarter + h * eighth : j * quarter + (h + 1) * eighth]
            own[:, columns] = block[:quarter]
            to_one[:eighth, columns] = at(2, 0).astype(BF16)
            to_one[eighth:, columns] = at(1, 0).astype(BF16)
            to_three[:eighth, columns] = at(2, 1).astype(BF16)
            to_three[eighth:, columns] = at(3, 1).astype(BF16)
            keep_one[:, columns] = at(1, 1)
            keep_three[:, columns] = at(3, 0)


def project_own(rows, gate_weight, up_weight, received):
    half = rows.shape[0] // 2
    units = gate_weight.shape[1]
    shapes = [
        jax.ShapeDtypeStruct((count, 2 * units), dtype)
        for count, dtype in ((half // 4, F32), (half // 4, BF16), (half // 4, BF16), (half // 8, F32), (half // 8, F32))
    ]
    return call(project_own_kernel, "project_own", shapes, [VMEM] * 4, [rows, gate_weight, up_weight, received], micros=4)


def relay_kernel(keep_one, keep_three, from_one, from_three, to_one, to_three):
    half = keep_one.shape[0]
    to_one[...] = (keep_one[...] + from_three[:half, :].astype(F32)).astype(BF16)
    to_three[...] = (keep_three[...] + from_one[:half, :].astype(F32)).astype(BF16)


def relay(parts, from_one, from_three):
    keeps = parts[3:]
    shape = jax.ShapeDtypeStruct(keeps[0].shape, BF16)
    return call(relay_kernel, "relay", [shape] * 2, [VMEM] * 4, [*keeps, from_one, from_three])


def sum_of(h, own, from_one, from_three, relay_one, relay_three):
    half = relay_one.shape[0]
    direct, relayed = (from_one, relay_three) if h == 0 else (from_three, relay_one)
    return own[h * half : (h + 1) * half, :] + direct[half:, :].astype(F32) + relayed[...].astype(F32)


def hidden_kernel(*refs):
    parts, out = refs[:-1], refs[-1]
    units = out.shape[1]
    half = out.shape[0] // 2
    for h in range(2):
        total = sum_of(h, *parts)
        gate, up = total[:, :units], total[:, units:]
        out[h * half : (h + 1) * half, :] = (gate / (1.0 + jnp.exp(-gate)) * up).astype(BF16)


def hidden_of(parts):
    rows, columns = parts[0].shape
    return call(
        hidden_kernel, "hidden", jax.ShapeDtypeStruct((rows, columns // 2), BF16), [VMEM] * 5, parts, many=False
    )


def down_kernel(first, rows, down_weight, own, to_one, to_three, keep_one, keep_three):
    half = rows.shape[0] // 2
    for outer in (2, 1, 3, 0):
        for pair in (0, 2):
            if first == "z":
                at = outer * 4 + pair
                weights = down_weight[:, at * LANES : (at + 2) * LANES]
            else:
                blocks = [pair * 4 + outer, (pair + 1) * 4 + outer]
                weights = jnp.concatenate([down_weight[:, at * LANES : (at + 1) * LANES] for at in blocks], axis=1)
            term = jnp.dot(rows[...], weights, preferred_element_type=F32)
            columns = slice(pair * LANES, (pair + 2) * LANES)
            if outer == 0:
                own[:, columns] = term
            elif outer == 1:
                to_one[half:, columns] = term[:half].astype(BF16)
                keep_one[:, columns] = term[half:]
            elif outer == 2:
                to_one[:half, columns] = term[:half].astype(BF16)
                to_three[:half, columns] = term[half:].astype(BF16)
            else:
                keep_three[:, columns] = term[:half]
                to_three[half:, columns] = term[half:].astype(BF16)


def down(first, rows, down_weight):
    count = rows.shape[0]
    width = down_weight.shape[1] // 4
    shapes = [
        jax.ShapeDtypeStruct((n, width), dtype)
        for n, dtype in ((count, F32), (count, BF16), (count, BF16), (count // 2, F32), (count // 2, F32))
    ]
    return call(
        functools.partial(down_kernel, first),
        "down_" + first,
        shapes,
        [VMEM, VMEM],
        [rows, down_weight],
        micros=4,
    )


def add_kernel(own, from_one, from_three, relay_one, relay_three, *outs):
    half = relay_one.shape[0]
    for h in range(2):
        total = sum_of(h, own, from_one, from_three, relay_one, relay_three)
        for i, out in enumerate(outs):
            out[h * half : (h + 1) * half, :] = total[:, i * LANES : (i + 1) * LANES].astype(out.dtype)


def add_line(parts):
    shapes = [jax.ShapeDtypeStruct((parts[0].shape[0], LANES), F32 if j == 0 else BF16) for j in range(4)]
    return call(add_kernel, "add_line", shapes, [VMEM] * 5, parts)


def send(axis, parts):
    return [parts[0]] + [from_wide(axis, bits, parts[bits]) for bits in (1, 2, 3)]


def last_kernel(place, *refs):
    parts, out = refs[:-1], refs[-1]
    y, c = place[2], place[3]
    rows = parts[0].shape[0]
    block = rows // 8
    for chunk in range(2):
        total = parts[4 * chunk][...]
        for k in range(1, 4):
            total = total + parts[4 * chunk + k][...].astype(F32)
        total = total.astype(BF16)
        for side in range(2):
            core = c if side == 0 else 1 - c
            for j in range(4):
                at = chunk * rows + ((y ^ j) * 2 + core) * block
                value = total[(side * 4 + j) * block : (side * 4 + j + 1) * block]
                out[pl.ds(pl.multiple_of(at, block), block), :] = value


def last(place, parts):
    shape = jax.ShapeDtypeStruct((2 * parts[0].shape[0], LANES), BF16)
    return call(last_kernel, "last", shape, [SMEM] + [VMEM] * 8, [place, *parts], many=False)


def body(tokens, gate_weight, up_weight, down_weight):
    wide, narrow = lax.axis_index("wide"), lax.axis_index("narrow")
    place = jnp.stack([wide // 4, wide % 4, narrow // 2, narrow % 2]).astype(jnp.int32)
    rows = tokens.shape[0] // 2
    both = range(2)
    tokens = after(tokens, place)
    lines = [line_of(axis, tokens[at * rows : (at + 1) * rows]) for at, axis in enumerate("zx")]
    lines[0] = after(lines[0], lines[1][1])
    stacks = [jnp.stack(line) for line in lines]
    nexts = [[from_wide(axis, bits, stack) for bits in (1, 3)] for axis, stack in zip("xz", stacks)]
    weights = load(False, place, *after((gate_weight, up_weight), stacks))
    nexts[0] = after(nexts[0], weights)
    bases = [assemble(axis, place, [stack, *near]) for axis, stack, near in zip("zx", stacks, nexts)]
    fars = [(from_wide(axis, 1, three[:2]), from_wide(axis, 3, one[2:])) for axis, (one, three) in zip("xz", nexts)]
    fars[0] = after(fars[0], bases[1])
    chunks = [assemble(axis, place, far, base) for axis, far, base in zip("zx", fars, bases)]
    others = []
    for at in both:
        others.append(project_other(after(chunks[at], *others), *weights))
    received = [swap(array) for array in others]
    parts = []
    for at in both:
        parts.append(project_own(after(chunks[at], others[1], *[p[0] for p in parts]), *weights, received[at]))
    def first_round(exchange, parts):
        return exchange(1, parts[1]), exchange(3, parts[2])

    def second_round(exchange, pair):
        return exchange(1, pair[0]), exchange(3, pair[1])

    together = lax.optimization_barrier
    half = parts[0][0].shape[0] // 2
    first = [first_round(from_y, p) for p in parts]
    (down_weight,) = load(True, place, after(down_weight, parts[1][0]))
    second = [second_round(from_y, relay(parts[0], *after(first[0], down_weight))), None]
    relayed = relay(parts[1], *first[1])
    second[0] = after(second[0], relayed[0])
    hidden = [hidden_of([parts[0][0], *first[0], *second[0]]), None]
    near = [[from_y(bits, hidden[0]) for bits in (1, 3)], None]
    second[1] = second_round(from_y, relayed)
    hidden[1] = hidden_of([parts[1][0], *first[1], *second[1]])
    near[1] = [from_y(bits, hidden[1]) for bits in (1, 3)]
    near[0] = after(near[0], hidden[1])
    far = [second_round(from_y, (near[0][1][:half], near[0][0][half:])), None]
    near[1], far[0] = together((near[1], far[0]))
    parts = []
    for at, axis in enumerate("zx"):
        if at == 1:
            far[1] = after(second_round(from_y, (near[1][1][:half], near[1][0][half:])), parts[0][0])
        rows_here = jnp.concatenate([hidden[at], near[at][0], *far[at], near[at][1]])
        parts.append(down(axis, jnp.concatenate([rows_here, swap(rows_here)]), down_weight))
    along = [functools.partial(from_wide, axis) for axis in "zx"]
    first = [first_round(exchange, p) for exchange, p in zip(along, parts)]
    second[0] = second_round(along[0], relay(parts[0], *after(first[0], parts[1][0])))
    relayed = relay(parts[1], *first[1])
    second[1] = second_round(along[1], relayed)
    final = send("x", add_line([parts[0][0], *first[0], *second[0]]))
    return last(place, final + send("z", add_line([parts[1][0], *first[1], *second[1]])))


def solution(mesh):
    return jax.shard_map(
        body,
        mesh=mesh,
        in_specs=(
            P(None, ("narrow", "wide")),
            P("narrow", "wide"),
            P("narrow", "wide"),
            P("wide", "narrow"),
        ),
        out_specs=P(None, ("narrow", "wide")),
        check_vma=False,
    )
```
